256 devices in a mesh: grp: 2 (over x_lo), seq: 64 (over x_hi, z, y), dp: 2 (over core).
Axes of the slice: x: 4 (x_hi: 2, x_lo: 2; x = x_hi * 2 + x_lo), y: 4, z: 8, core: 2. Of those that a mesh axis runs over, the one named last changes fastest.
Arguments:
- gen_input: bfloat16 [2, 4096, 64], P('dp', 'seq'), may hold values from -6 to 6
- noise: bfloat16 [2, 4096, 64], P('dp', 'seq'), may hold values from -6 to 6
- gen_step: int32 [2], P('dp'), may hold values from 0 to 999
- critic_step: int32 [2], P('dp'), may hold values from 0 to 999
- gen_in: bfloat16 [64, 5120], replicated, may hold values from -0.75 to 0.75
- gen_out: bfloat16 [5120, 64], replicated, may hold values from -0.078125 to 0.078125
- critic_embed: bfloat16 [2, 64, 5120], P('grp'), may hold values from -0.75 to 0.75
- critic_qkv: bfloat16 [2, 64, 2560, 384], P('grp', 'seq'), may hold values from -0.078125 to 0.078125
- critic_out: bfloat16 [2, 64, 64, 64], P('grp', 'seq'), may hold values from -1.5 to 1.5
Outputs:
- dmd_grad: float32 [2, 4096, 64], P('dp', 'seq')
- grad_in: float32 [64, 5120], replicated
- grad_out: float32 [5120, 64], replicated
The draws below stay inside these ranges and needn't reach their ends.
All inputs are finite; a program needn't handle non-finite values. Where the reference program divides by a largest or mean magnitude, that divisor is 1e-20 or more.
Results may differ from the reference program's by a relative error of at most 0.0034.
Values may be sent and summed in bfloat16 or wider, within the bound.
A program may use at most 128 MiB of HBM per device.

```python
import jax
import jax.numpy as jnp
from jax import lax

D = 5120
HD = 128
LAT = 64
NT = 1000
HEADS = 32
L = 4096
CLIPS = 2


def steps_of(own_key, extent, pieces, low, top_value):
    def one(dim, blocks):
        steps = jax.random.uniform(jax.random.fold_in(jax.random.fold_in(own_key, 6), dim), (blocks,), jnp.float32, low / len(pieces), top_value / len(pieces))
        return jnp.repeat(jnp.exp(steps), extent[dim] // blocks).reshape((-1,) + (1,) * (len(extent) - dim - 1))

    gain = one(*pieces[0])
    for cut in pieces[1:]:
        gain = gain * one(*cut)
    return gain


def bell_draw(own_key, shape, scale, limit, split=(), dtype=jnp.bfloat16):
    result = scale * jax.random.normal(own_key, shape, jnp.float32)
    if split:
        result = result * steps_of(own_key, shape, split, -0.22, 0.18)
    return jnp.clip(result, -limit, limit).astype(dtype)


def setup_inputs(seed: int = 0) -> dict:
    arg_keys = jax.random.split(jax.random.key(seed), 10)
    gen_input = bell_draw(arg_keys[0], (CLIPS, L, LAT), 1.0, 6.0, ((0, 2), (1, 64)))
    noise = bell_draw(arg_keys[1], (CLIPS, L, LAT), 1.0, 6.0, ((0, 2), (1, 64)))
    gen_step = jax.random.randint(arg_keys[2], (CLIPS,), 0, NT).astype(jnp.int32)
    critic_step = jax.random.randint(arg_keys[3], (CLIPS,), 0, NT).astype(jnp.int32)
    gen_in = bell_draw(arg_keys[4], (LAT, D), LAT ** -0.5, 0.75)
    gen_out = bell_draw(arg_keys[5], (D, LAT), D ** -0.5, 0.078125)
    critic_embed = bell_draw(arg_keys[6], (2, LAT, D), LAT ** -0.5, 0.75, ((0, 2),))
    critic_qkv = bell_draw(arg_keys[7], (2, 2 * HEADS, D // 2, 3 * HD), D ** -0.5, 0.078125, ((0, 2), (1, 64)))
    critic_out = bell_draw(arg_keys[8], (2, 2 * HEADS, HD // 2, LAT), 16 ** -0.5, 1.5, ((0, 2), (1, 64)))
    return {"gen_input": gen_input, "noise": noise, "gen_step": gen_step, "critic_step": critic_step, "gen_in": gen_in, "gen_out": gen_out, "critic_embed": critic_embed, "critic_qkv": critic_qkv, "critic_out": critic_out}


SHIFT_VALUE = 5.0
EPS_NORM = 1e-06
EPS_SPREAD = 1e-06

def sigma_of(step):
    frac = (step.astype(jnp.float32) + 1.0) / NT
    return SHIFT_VALUE * frac / (1.0 + (SHIFT_VALUE - 1.0) * frac)

def rms_scaled(pre):
    return pre * lax.rsqrt(lax.optimization_barrier(jnp.mean(pre * pre, axis=-1, keepdims=True)) + EPS_NORM)

def norm_gelu(pre):
    return jax.nn.gelu(rms_scaled(pre), approximate=True)

def critic_velocity(noisy, embed, qkv_weight, out_weight):
    features = jax.nn.gelu(jnp.dot(noisy, embed, preferred_element_type=jnp.float32), approximate=True)
    normed = rms_scaled(features).astype(jnp.bfloat16)
    half_width = normed.shape[1] // 2
    pairs = qkv_weight.reshape(HEADS, 2, half_width, 3 * HD)
    outs = out_weight.reshape(HEADS, HD, LAT)

    def one_head(items):
        weight_pair, out_full = items
        proj = (jnp.dot(normed[:, :half_width], weight_pair[0], preferred_element_type=jnp.float32) + jnp.dot(normed[:, half_width:], weight_pair[1], preferred_element_type=jnp.float32)).astype(jnp.bfloat16)
        query = proj[:, :HD]
        keys = proj[:, HD:2 * HD]
        values = proj[:, 2 * HD:]
        scores = jnp.dot(query, keys.T, preferred_element_type=jnp.float32) * HD ** (-0.5)
        probs = jax.nn.softmax(scores, axis=-1).astype(jnp.bfloat16)
        attended = jnp.dot(probs, values, preferred_element_type=jnp.float32).astype(jnp.bfloat16)
        return jnp.dot(attended, out_full, preferred_element_type=jnp.float32)
    return lax.optimization_barrier(jnp.sum(lax.map(one_head, (pairs, outs)), axis=0))

def reference(gen_input, noise, gen_step, critic_step, gen_in, gen_out, critic_embed, critic_qkv, critic_out):
    grad_in = jnp.zeros((LAT, D), jnp.float32)
    grad_out = jnp.zeros((D, LAT), jnp.float32)
    results = []
    for clip in range(CLIPS):
        gen_sigma = sigma_of(gen_step[clip])
        crit_sigma = sigma_of(critic_step[clip])
        latent = gen_input[clip]
        pre = jnp.dot(latent, gen_in, preferred_element_type=jnp.float32)
        hidden = norm_gelu(pre).astype(jnp.bfloat16)
        clean = latent.astype(jnp.float32) - gen_sigma * jnp.dot(hidden, gen_out, preferred_element_type=jnp.float32)
        noisy = ((1.0 - crit_sigma) * clean + crit_sigma * noise[clip].astype(jnp.float32)).astype(jnp.bfloat16)
        teacher_vel = critic_velocity(noisy, critic_embed[0], critic_qkv[0], critic_out[0])
        fake_vel = critic_velocity(noisy, critic_embed[1], critic_qkv[1], critic_out[1])
        teacher_clean = noisy.astype(jnp.float32) - crit_sigma * teacher_vel
        spread = jnp.mean(jnp.abs(clean - teacher_clean)) + EPS_SPREAD
        dmd = -crit_sigma * (fake_vel - teacher_vel) / spread
        results.append(dmd)
        dvel = (-gen_sigma * dmd).astype(jnp.bfloat16)
        grad_out = grad_out + jnp.dot(hidden.T, dvel, preferred_element_type=jnp.float32)
        dhidden = jnp.dot(dvel, gen_out.T, preferred_element_type=jnp.float32)
        unused, pullback = jax.vjp(norm_gelu, pre)
        dpre = pullback(dhidden)[0].astype(jnp.bfloat16)
        grad_in = grad_in + jnp.dot(latent.T, dpre, preferred_element_type=jnp.float32)
    return (jnp.stack(results, axis=0), grad_in, grad_out)
```

```python
import functools

import jax
import jax.numpy as jnp
from jax import lax
from jax.experimental import pallas as pl
from jax.experimental.pallas import tpu as pltpu
from jax.sharding import PartitionSpec as P

F32 = jnp.float32
BF16 = jnp.bfloat16
NT = 1000
D = 5120
HALF = 2560
LAT = 64
HD = 128
ROWS = 2048
CHUNK = 1280
SHIFT_VALUE = 5.0
EPS_NORM = 1e-06
EPS_SPREAD = 1e-06
COUNT = 4096 * 64
GA = 0.7978845608028654
GB = GA * 0.044715
SCORE_SCALE = 1.4426950408889634 * HD**-0.5
MESH = pl.DeviceIdType.MESH
CONTRACT_LAST = (((1,), (1,)), ((), ()))


def dot(a, b):
    return jnp.dot(a, b, preferred_element_type=F32)


def dot_nt(a, b):
    return lax.dot_general(a, b, CONTRACT_LAST, preferred_element_type=F32)


def place():
    b = lax.axis_index("grp")
    s = lax.axis_index("seq")
    c = lax.axis_index("dp")
    return b, s // 32, (s // 4) % 8, s % 4, c


def seq_of(xh, z, y):
    return xh * 32 + z * 4 + y


def remote(src, dst, send, recv, device):
    return pltpu.make_async_remote_copy(
        src_ref=src, dst_ref=dst, send_sem=send, recv_sem=recv, device_id=device, device_id_type=MESH
    )


def greet(barrier, device):
    pl.semaphore_signal(barrier, inc=1, device_id=device, device_id_type=MESH)


def sigma_rows(step_ref):
    step = jnp.full((8, 128), step_ref[0], jnp.int32).astype(F32)
    frac = (step + 1.0) / NT
    return (SHIFT_VALUE * frac / (1.0 + (SHIFT_VALUE - 1.0) * frac))[0:1, :]


def split2(value):
    high = value.astype(BF16)
    low = (value - high.astype(F32)).astype(BF16)
    return high, low


def pack(value):
    return jnp.concatenate([value[:32], value[32:]], axis=1)


def generate_kernel(
    lat_ref, noise_ref, gs_ref, cs_ref, gin_ref, gout_ref,
    rows_out, clean_out, noisy_out, early_out, q_out,
    pre_s, mine_s, rows_s, send, recv,
):
    b, xh, z, y, c = place()
    j = y % 2
    y_high = y // 2
    is_self = jnp.logical_and(j == c, y_high == c)
    barrier = pltpu.get_barrier_semaphore()
    for k in range(4):
        source_self = jnp.logical_and(is_self, jnp.logical_and(xh == k // 2, j == k % 2))

        @pl.when(jnp.logical_not(source_self))
        def _():
            greet(barrier, (b, seq_of(k // 2, z, 2 * c + k % 2), j))

    for d in range(1, 8):
        greet(barrier, (b, seq_of(xh, (z + d) % 8, y), c))

    sg = sigma_rows(gs_ref)
    sc = sigma_rows(cs_ref)
    lat = lat_ref[...]
    squares = jnp.zeros((64, 128), F32)
    width = 512
    for t in range(D // width):
        cols = slice(t * width, (t + 1) * width)
        pre = dot(lat, gin_ref[:, cols])
        pre_s[:, cols] = pre
        sq = pre * pre
        for u in range(width // 128):
            squares = squares + sq[:, u * 128 : (u + 1) * 128]
    scale = lax.rsqrt(jnp.sum(squares, axis=-1, keepdims=True) / D + EPS_NORM)
    out = jnp.zeros((64, LAT), F32)
    qv = jnp.zeros((64, LAT), F32)
    for t in range(D // width):
        cols = slice(t * width, (t + 1) * width)
        n = pre_s[:, cols] * scale
        n2 = n * n
        th = jnp.tanh(n * (GA + GB * n2))
        hidden = (0.5 * n * (1.0 + th)).astype(BF16)
        slope = 0.5 * (1.0 + th) + 0.5 * n * (1.0 - th * th) * (GA + 3.0 * GB * n2)
        weight = gout_ref[cols, :]
        out = out + dot(hidden, weight)
        qv = qv + dot((slope * n).astype(BF16), weight)
    lat_f = lat.astype(F32)
    clean = lat_f - sg[:, :64] * out
    noisy = ((1.0 - sc[:, :64]) * clean + sc[:, :64] * noise_ref[...].astype(F32)).astype(BF16)
    mine = pack(noisy)
    mine_s[...] = mine

    slot = xh * 2 + j

    @pl.when(is_self)
    def _():
        rows_s[z, slot] = mine

    pl.semaphore_wait(barrier, 11 - is_self.astype(jnp.int32))

    def first(k):
        return remote(
            mine_s, rows_s.at[z, slot], send.at[k], recv.at[slot],
            (b, seq_of(k // 2, z, c + 2 * (k % 2)), y_high),
        )

    def target_self(k):
        return jnp.logical_and(is_self, jnp.logical_and(xh == k // 2, y == c + 2 * (k % 2)))

    for k in range(4):
        @pl.when(jnp.logical_not(target_self(k)))
        def _():
            first(k).start()

    clean_out[...] = pack(clean)
    noisy_out[...] = mine
    high, low = split2(lat_f * scale)
    early = jnp.concatenate([high, low], axis=1)
    early_out[...] = jnp.where(b == 0, early[:32], early[32:])
    q_out[...] = jnp.where(b == 0, qv[:32], qv[32:])

    for k in range(4):
        source_self = jnp.logical_and(is_self, jnp.logical_and(xh == k // 2, j == k % 2))

        @pl.when(jnp.logical_not(source_self))
        def _():
            remote(mine_s, rows_s.at[z, k], send.at[k], recv.at[k], (b, seq_of(xh, z, y), c)).wait_recv()

    def second(d):
        return remote(
            rows_s.at[z], rows_s.at[z], send.at[3 + d], recv.at[3 + d],
            (b, seq_of(xh, (z + d) % 8, y), c),
        )

    for d in range(1, 8):
        second(d).start()
    for d in range(1, 8):
        from_z = (z + 8 - d) % 8
        remote(
            rows_s.at[z], rows_s.at[from_z], send.at[3 + d], recv.at[3 + d],
            (b, seq_of(xh, from_z, y), c),
        ).wait_recv()
    rows_out[...] = rows_s[...]
    for k in range(4):
        @pl.when(jnp.logical_not(target_self(k)))
        def _():
            first(k).wait_send()
    for d in range(1, 8):
        second(d).wait_send()


def vmem(n):
    return [pl.BlockSpec(memory_space=pltpu.VMEM)] * n


def generate(latent, noise, gen_step, critic_step, gen_in, gen_out):
    smem = pl.BlockSpec(memory_space=pltpu.SMEM)
    return pl.pallas_call(
        generate_kernel,
        out_shape=(
            jax.ShapeDtypeStruct((8, 4, 32, 128), BF16),
            jax.ShapeDtypeStruct((32, 128), F32),
            jax.ShapeDtypeStruct((32, 128), BF16),
            jax.ShapeDtypeStruct((32, 128), BF16),
            jax.ShapeDtypeStruct((32, 64), F32),
        ),
        in_specs=vmem(2) + [smem, smem] + vmem(2),
        out_specs=tuple(vmem(5)),
        scratch_shapes=[
            pltpu.VMEM((64, D), F32),
            pltpu.VMEM((32, 128), BF16),
            pltpu.VMEM((8, 4, 32, 128), BF16),
            pltpu.SemaphoreType.DMA((11,)),
            pltpu.SemaphoreType.DMA((11,)),
        ],
        compiler_params=pltpu.CompilerParams(
            collective_id=0, has_side_effects=True, vmem_limit_bytes=32 << 20
        ),
        cost_estimate=pl.CostEstimate(flops=200_000_000, bytes_accessed=30_000_000, transcendentals=700_000),
    )(latent, noise, gen_step, critic_step, gen_in, gen_out)


TILE = 256


def features(x):
    return x + x * jnp.tanh(x * (GA + GB * (x * x)))


def project_chunk(rows_ref, embed, weight, acc, ssq):
    def activate(t):
        side, part = t // 4, t % 4
        x = dot(rows_ref[part * TILE : (part + 1) * TILE, side * 64 : (side + 1) * 64], embed)
        e = features(x)
        squares = e * e
        total = squares[:, :128]
        for u in range(1, CHUNK // 128):
            total = total + squares[:, u * 128 : (u + 1) * 128]
        ssq[t * TILE : (t + 1) * TILE, :] += total
        return e.astype(BF16)

    def accumulate(t, e):
        acc[t * TILE : (t + 1) * TILE, :] += dot(e, weight)

    before = activate(0)
    for t in range(1, 8):
        now = activate(t)
        accumulate(t - 1, before)
        before = now
    accumulate(7, before)


def embed_columns(embed_ref, start):
    return embed_ref[:, pl.ds(pl.multiple_of(start, 128), CHUNK)]


def project_own_kernel(rows_ref, embed_ref, weight_ref, acc, ssq):
    j = lax.axis_index("seq") % 2
    f = pl.program_id(0)

    @pl.when(f == 0)
    def _():
        acc[...] = jnp.zeros_like(acc)
        ssq[...] = jnp.zeros_like(ssq)

    project_chunk(rows_ref, embed_columns(embed_ref, j * HALF + f * CHUNK), weight_ref[...], acc, ssq)


def project_own(rows, embed, weight):
    whole = lambda *shape: pl.BlockSpec(shape, lambda f: (0,) * len(shape))
    return pl.pallas_call(
        project_own_kernel,
        grid=(2,),
        in_specs=[whole(1024, 128), whole(64, D), pl.BlockSpec((CHUNK, 3 * HD), lambda f: (f, 0))],
        out_specs=(whole(ROWS, 3 * HD), whole(ROWS, 128)),
        out_shape=(
            jax.ShapeDtypeStruct((ROWS, 3 * HD), F32),
            jax.ShapeDtypeStruct((ROWS, 128), F32),
        ),
        compiler_params=pltpu.CompilerParams(vmem_limit_bytes=48 << 20),
        cost_estimate=pl.CostEstimate(flops=9_000_000_000, bytes_accessed=30_000_000, transcendentals=5_000_000),
    )(rows, embed, weight)


def project_other_kernel(acc_in, ssq_in, rows_ref, embed_ref, first_ref, second_ref, qkv_ref, acc, ssq):
    j = lax.axis_index("seq") % 2
    c = lax.axis_index("dp")
    acc[...] = acc_in[...]
    ssq[...] = ssq_in[...]
    base = (1 - j) * HALF
    project_chunk(rows_ref, embed_columns(embed_ref, base + c * CHUNK), first_ref[...], acc, ssq)
    project_chunk(rows_ref, embed_columns(embed_ref, base + (1 - c) * CHUNK), second_ref[...], acc, ssq)
    for t in range(8):
        rows = slice(t * TILE, (t + 1) * TILE)
        mean = jnp.sum(ssq[rows, :], axis=-1, keepdims=True) / D
        qkv_ref[rows, :] = (acc[rows, :] * lax.rsqrt(mean + 4.0 * EPS_NORM)).astype(BF16)


def project_other(acc, ssq, rows, embed, first, second):
    return pl.pallas_call(
        project_other_kernel,
        in_specs=vmem(6),
        out_specs=vmem(1)[0],
        out_shape=jax.ShapeDtypeStruct((ROWS, 3 * HD), BF16),
        scratch_shapes=[pltpu.VMEM((ROWS, 3 * HD), F32), pltpu.VMEM((ROWS, 128), F32)],
        compiler_params=pltpu.CompilerParams(vmem_limit_bytes=48 << 20),
        cost_estimate=pl.CostEstimate(flops=9_000_000_000, bytes_accessed=30_000_000, transcendentals=5_000_000),
    )(acc, ssq, rows, embed, first, second)


def attend_kernel(qkv_ref, kv_ref, mine_ref, other_ref, out_ref, kk, vv, uu):
    j = lax.axis_index("seq") % 2
    keys = qkv_ref[:, HD : 2 * HD]
    kk[:ROWS, :HD] = keys
    kk[:ROWS, HD:] = keys
    keys = kv_ref[:, :HD]
    kk[ROWS:, :HD] = keys
    kk[ROWS:, HD:] = keys
    vv[:ROWS, :HD] = qkv_ref[:, 2 * HD :]
    vv[ROWS:, :HD] = kv_ref[:, HD:]
    vv[:, HD:] = jnp.ones((2 * ROWS, HD), BF16)
    mine = mine_ref[...]
    other = other_ref[...]
    full = jnp.concatenate([jnp.where(j == 0, mine, other), jnp.where(j == 0, other, mine)], axis=0)
    none = jnp.zeros((HD, LAT), BF16)
    uu[:HD, :] = jnp.concatenate([full, none], axis=1)
    uu[HD:, :] = jnp.concatenate([none, full], axis=1)

    def scores(t):
        low = qkv_ref[t * 128 : (t + 1) * 128, :HD]
        high = qkv_ref[1024 + t * 128 : 1024 + (t + 1) * 128, :HD]
        query = jnp.concatenate([low, high], axis=0).astype(F32) * SCORE_SCALE
        return dot_nt(jnp.concatenate(split2(query), axis=1), kk[...])

    def finish(t, s):
        top = jnp.max(s, axis=-1, keepdims=True)
        probs = jnp.exp2(s - top).astype(BF16)
        got = dot(probs, vv[...])
        attended = (got[:, :HD] / got[:, HD:]).astype(BF16)
        both = jnp.concatenate([attended[:128], attended[128:]], axis=1)
        out_ref[t] = dot(both, uu[...]).astype(BF16)

    before = scores(0)
    for t in range(1, 8):
        now = scores(t)
        finish(t - 1, before)
        before = now
    finish(7, before)


def attend(qkv, kv, mine, other):
    return pl.pallas_call(
        attend_kernel,
        in_specs=vmem(4),
        out_specs=vmem(1)[0],
        out_shape=jax.ShapeDtypeStruct((8, 128, 128), BF16),
        scratch_shapes=[
            pltpu.VMEM((2 * ROWS, 2 * HD), BF16),
            pltpu.VMEM((2 * ROWS, 2 * HD), BF16),
            pltpu.VMEM((2 * HD, 128), BF16),
        ],
        compiler_params=pltpu.CompilerParams(vmem_limit_bytes=56 << 20),
    )(qkv, kv, mine, other)


E_Z, E_Y, A_Z, B_X, L_Z, L_Y, X_X, F_Z, F_Y, F_C, N_SEM = 0, 8, 12, 20, 28, 36, 40, 48, 56, 60, 64


def finish_kernel(
    vel_ref, clean_ref, noisy_ref, early_ref, q_ref, gs_ref, cs_ref, gi_ref, go_ref,
    dmd_out, grads_out,
    eb, lb, arrive_a, part_b, arrive_b, n_s, slope_s, hid_s, piece_s, arrive_x, fin, send, recv,
):
    b, xh, z, y, c = place()
    j = y % 2
    y_high = y // 2
    is_self = jnp.logical_and(j == c, y_high == c)
    barrier = pltpu.get_barrier_semaphore()

    def at_z(d):
        return (b, seq_of(xh, (z + d) % 8, y), c)

    def at_y(d):
        return (b, seq_of(xh, z, (y + d) % 4), c)

    def at_x(k):
        return ((b + k // 4) % 2, seq_of((xh + k // 2 % 2) % 2, z, y), (c + k % 2) % 2)

    def source_b_self(k):
        return jnp.logical_and(
            is_self, jnp.logical_and(b == k // 4, jnp.logical_and(xh == k // 2 % 2, y_high == k % 2))
        )

    def target_b_self(k):
        return jnp.logical_and(
            is_self, jnp.logical_and(b == k // 4, jnp.logical_and(xh == k // 2 % 2, j == k % 2))
        )

    for d in range(1, 8):
        greet(barrier, at_z(d))
        greet(barrier, at_x(d))
    for d in range(1, 4):
        greet(barrier, at_y(d))
    for k in range(8):
        @pl.when(jnp.logical_not(source_b_self(k)))
        def _():
            greet(barrier, (k // 4, seq_of(k // 2 % 2, z, c + 2 * (k % 2)), y_high))
    eb[0, 0] = early_ref[...]
    pl.semaphore_wait(barrier, 25 - is_self.astype(jnp.int32))

    def along_z(buf, base, d):
        return remote(buf.at[0, 0], buf.at[0, d], send.at[base + d], recv.at[base + d], at_z(d))

    def along_y(buf, base, d):
        return remote(buf.at[0], buf.at[d], send.at[base + d], recv.at[base + d], at_y(d))

    def vel_copy(d):
        return remote(
            vel_ref.at[(z + d) % 8], arrive_a.at[d - 1], send.at[A_Z + d], recv.at[A_Z + d], at_z(d)
        )

    for d in range(1, 8):
        along_z(eb, E_Z, d).start()
    for d in range(1, 8):
        vel_copy(d).start()
    for d in range(1, 8):
        along_z(eb, E_Z, d).wait_recv()
    for d in range(1, 4):
        along_y(eb, E_Y, d).start()

    total = vel_ref[z].astype(F32)
    for d in range(1, 8):
        vel_copy(d).wait_recv()
        total = total + arrive_a[d - 1].astype(F32)
    for k in range(4):
        part_b[k] = total[k * 32 : (k + 1) * 32]
    slot_b = b * 4 + xh * 2 + y_high

    def part_copy(k):
        device = (k // 4, seq_of(k // 2 % 2, z, 2 * c + k % 2), j)
        return remote(part_b.at[k % 4], arrive_b.at[slot_b], send.at[B_X + k], recv.at[B_X + slot_b], device)

    for k in range(8):
        @pl.when(jnp.logical_not(target_b_self(k)))
        def _():
            part_copy(k).start()

        @pl.when(target_b_self(k))
        def _():
            arrive_b[slot_b] = part_b[k % 4]

    for d in range(1, 4):
        along_y(eb, E_Y, d).wait_recv()
    early = eb[...].reshape(1024, 128)
    n = dot_nt(gi_ref[...], early)
    n2 = n * n
    th = jnp.tanh(n * (GA + GB * n2))
    n_s[...] = n
    hid_s[...] = (0.5 * n * (1.0 + th)).astype(BF16)
    slope_s[...] = 0.5 * (1.0 + th) + 0.5 * n * (1.0 - th * th) * (GA + 3.0 * GB * n2)

    for k in range(8):
        @pl.when(jnp.logical_not(source_b_self(k)))
        def _():
            remote(
                part_b.at[k % 4], arrive_b.at[k], send.at[B_X + k], recv.at[B_X + k],
                (b, seq_of(xh, z, y), c),
            ).wait_recv()

    sg = sigma_rows(gs_ref)
    sc = sigma_rows(cs_ref)
    teacher = arrive_b[0] + arrive_b[1] + arrive_b[2] + arrive_b[3]
    fake = arrive_b[4] + arrive_b[5] + arrive_b[6] + arrive_b[7]
    gap = fake - teacher
    away = jnp.abs(clean_ref[...] - (noisy_ref[...].astype(F32) - sc * teacher))
    my_gap = jnp.where(b == 0, gap[:, :64], gap[:, 64:])
    my_away = jnp.where(b == 0, away[:, :64], away[:, 64:])
    away_row = jnp.sum(my_away, axis=-1, keepdims=True)
    rbar = jnp.sum(my_gap * q_ref[...], axis=-1, keepdims=True) / D
    r_high, r_low = split2(rbar)
    a_high, a_low = split2(away_row)
    a_rest = (away_row - a_high.astype(F32) - a_low.astype(F32)).astype(BF16)
    lane = lax.broadcasted_iota(jnp.int32, (32, 64), 1)
    extra = jnp.zeros((32, 64), F32)
    for at, value in enumerate((r_high, r_low, a_high, a_low, a_rest)):
        extra = jnp.where(lane == at, value.astype(F32), extra)
    lb[0, 0] = jnp.concatenate([my_gap, extra], axis=1).astype(BF16)

    for d in range(1, 8):
        along_z(lb, L_Z, d).start()
    for d in range(1, 8):
        along_z(lb, L_Z, d).wait_recv()
    for d in range(1, 4):
        along_y(lb, L_Y, d).start()
    for d in range(1, 4):
        along_y(lb, L_Y, d).wait_recv()
    late = lb[...].reshape(1024, 128)
    lane = lax.broadcasted_iota(jnp.int32, (16, 128), 1)
    pick = jnp.where(jnp.logical_or(lane == 64, lane == 65), 1.0, 0.0).astype(BF16)
    rbar_all = dot_nt(pick, late)[0:1, :]
    away_all = dot(jnp.ones((16, 1024), BF16), late)[0:1, :]
    lane1 = lax.broadcasted_iota(jnp.int32, (1, 128), 1)
    away_sum = jnp.sum(
        jnp.where(jnp.logical_and(lane1 >= 66, lane1 <= 68), away_all, 0.0), axis=-1, keepdims=True
    )
    dpre = (slope_s[...] * dot_nt(go_ref[...], late) - n_s[...] * rbar_all).astype(BF16)
    grad_in = dot(dpre, early)
    grad_out = dot(hid_s[...], late)
    piece = jnp.concatenate([grad_in[:, :64] + grad_in[:, 64:], grad_out[:, :64]], axis=1)
    row8 = lax.broadcasted_iota(jnp.int32, (8, 128), 0)
    extra8 = jnp.where(row8 == 0, away_sum, sg * sc)
    for p in range(2):
        piece_s[p, :80] = piece[p * 80 : (p + 1) * 80]
        piece_s[p, 80:] = extra8

    def piece_copy(k):
        return remote(
            piece_s.at[(c + k % 2) % 2], arrive_x.at[k], send.at[X_X + k], recv.at[X_X + k], at_x(k)
        )

    for k in range(1, 8):
        piece_copy(k).start()
    arrive_x[0] = piece_s[c]
    for k in range(1, 8):
        piece_copy(k).wait_recv()
    same = arrive_x[0] + arrive_x[2] + arrive_x[4] + arrive_x[6]
    cross = arrive_x[1] + arrive_x[3] + arrive_x[5] + arrive_x[7]
    spread = same[80:81] / COUNT + EPS_SPREAD
    spread_cross = cross[80:81] / COUNT + EPS_SPREAD
    result = (0.25 * same[81:82] / spread) * same[:80] + (0.25 * cross[81:82] / spread_cross) * cross[:80]
    fin[y, z, c] = result.astype(BF16)
    dmd = -sc * gap / spread
    dmd_out[:32] = dmd[:, :64]
    dmd_out[32:] = dmd[:, 64:]

    def out_z(d):
        at = fin.at[y, z, c]
        return remote(at, at, send.at[F_Z + d], recv.at[F_Z + d], at_z(d))

    def out_y(d):
        at = fin.at[y, :, c]
        return remote(at, at, send.at[F_Y + d], recv.at[F_Y + d], at_y(d))

    def out_core(d):
        at = fin.at[(y + 4 - d) % 4, :, c]
        return remote(at, at, send.at[F_C + d], recv.at[F_C + d], (b, seq_of(xh, z, y), 1 - c))

    for d in range(1, 8):
        out_z(d).start()
    for d in range(1, 8):
        at = fin.at[y, (z + 8 - d) % 8, c]
        remote(at, at, send.at[F_Z + d], recv.at[F_Z + d], at_z(d)).wait_recv()
    for d in range(1, 4):
        out_y(d).start()
    out_core(0).start()
    for d in range(1, 4):
        at = fin.at[(y + 4 - d) % 4, :, c]
        remote(at, at, send.at[F_Y + d], recv.at[F_Y + d], at_y(d)).wait_recv()
        out_core(d).start()
    for d in range(4):
        at = fin.at[(y + 4 - d) % 4, :, 1 - c]
        remote(at, at, send.at[F_C + d], recv.at[F_C + d], (b, seq_of(xh, z, y), 1 - c)).wait_recv()
    grads_out[...] = fin[...]

    for d in range(1, 8):
        along_z(eb, E_Z, d).wait_send()
        vel_copy(d).wait_send()
        along_z(lb, L_Z, d).wait_send()
        piece_copy(d).wait_send()
        out_z(d).wait_send()
    for d in range(1, 4):
        along_y(eb, E_Y, d).wait_send()
        along_y(lb, L_Y, d).wait_send()
        out_y(d).wait_send()
    for d in range(4):
        out_core(d).wait_send()
    for k in range(8):
        @pl.when(jnp.logical_not(target_b_self(k)))
        def _():
            part_copy(k).wait_send()


def finish(vel, clean, noisy, early, qv, gen_step, critic_step, gi, go):
    smem = pl.BlockSpec(memory_space=pltpu.SMEM)
    return pl.pallas_call(
        finish_kernel,
        out_shape=(
            jax.ShapeDtypeStruct((64, 64), F32),
            jax.ShapeDtypeStruct((4, 8, 2, 80, 128), BF16),
        ),
        in_specs=vmem(5) + [smem, smem] + vmem(2),
        out_specs=tuple(vmem(2)),
        scratch_shapes=[
            pltpu.VMEM((4, 8, 32, 128), BF16),
            pltpu.VMEM((4, 8, 32, 128), BF16),
            pltpu.VMEM((7, 128, 128), BF16),
            pltpu.VMEM((4, 32, 128), F32),
            pltpu.VMEM((8, 32, 128), F32),
            pltpu.VMEM((160, 1024), F32),
            pltpu.VMEM((160, 1024), F32),
            pltpu.VMEM((160, 1024), BF16),
            pltpu.VMEM((2, 88, 128), F32),
            pltpu.VMEM((8, 88, 128), F32),
            pltpu.VMEM((4, 8, 2, 80, 128), BF16),
            pltpu.SemaphoreType.DMA((N_SEM,)),
            pltpu.SemaphoreType.DMA((N_SEM,)),
        ],
        compiler_params=pltpu.CompilerParams(
            collective_id=1, has_side_effects=True, vmem_limit_bytes=32 << 20
        ),
    )(vel, clean, noisy, early, qv, gen_step, critic_step, gi, go)


def per_device(
    gen_input, noise, gen_step, critic_step, gen_in, gen_out, critic_embed, critic_qkv, critic_out
):
    b, xh, z, y, c = place()
    weight = critic_qkv[0, 0]
    mine = critic_out[0, 0]
    embed = critic_embed[0]
    swap_seq = [(i, i ^ 1) for i in range(lax.axis_size("seq"))]
    half = lax.dynamic_slice_in_dim(weight, c * CHUNK, CHUNK, 0)
    first, other = lax.ppermute((half, mine), "seq", swap_seq)
    second = lax.ppermute(first, "dp", [(0, 1), (1, 0)])
    rows, clean, noisy, early, qv = generate(gen_input[0], noise[0], gen_step, critic_step, gen_in, gen_out)
    rows = rows.reshape(1024, 128)
    acc, ssq = project_own(rows, embed, weight)
    qkv = project_other(acc, ssq, rows, embed, first, second)
    kv = lax.ppermute(qkv[:, HD:], "dp", [(0, 1), (1, 0)])
    vel = attend(qkv, kv, mine, other)
    at = (y * 8 + z) * 160
    gi = lax.dynamic_slice_in_dim(gen_in, at, 160, 1).T
    gi = jnp.concatenate([gi, gi], axis=1)
    go = lax.dynamic_slice_in_dim(gen_out, at, 160, 0)
    go = jnp.concatenate([go, jnp.zeros_like(go)], axis=1)
    dmd, grads = finish(vel, clean, noisy, early, qv, gen_step, critic_step, gi, go)
    grads = grads.reshape(D, 128).astype(F32)
    return (dmd[None], grads[:, :64].T, grads[:, 64:])


def solution(mesh):
    return jax.shard_map(
        per_device,
        mesh=mesh,
        in_specs=(
            P("dp", "seq", None),
            P("dp", "seq", None),
            P("dp"),
            P("dp"),
            P(),
            P(),
            P("grp", None, None),
            P("grp", "seq", None, None),
            P("grp", "seq", None, None),
        ),
        out_specs=(P("dp", "seq", None), P(), P()),
        check_vma=False,
    )
```

```python
import jax
import jax.numpy as jnp
from jax import lax
from jax.experimental import pallas as pl
from jax.experimental.pallas import tpu as pltpu
from jax.sharding import PartitionSpec as P

F32 = jnp.float32
BF16 = jnp.bfloat16
NT = 1000
D = 5120
HALF = 2560
LAT = 64
HD = 128
ROWS = 2048
TILE = 256
PART = 640
CHUNK = 1280
SHIFT_VALUE = 5.0
EPS_NORM = 1e-06
EPS_SPREAD = 1e-06
COUNT = 4096 * 64
GA = 0.7978845608028654
GB = GA * 0.044715
SCORE_SCALE = 1.4426950408889634 * HD**-0.5
MESH = pl.DeviceIdType.MESH
CONTRACT_LAST = (((1,), (1,)), ((), ()))


def dot(a, b):
    return jnp.dot(a, b, preferred_element_type=F32)


def dot_nt(a, b):
    return lax.dot_general(a, b, CONTRACT_LAST, preferred_element_type=F32)


def place():
    b = lax.axis_index("grp")
    s = lax.axis_index("seq")
    c = lax.axis_index("dp")
    return b, s // 32, (s // 4) % 8, s % 4, c


def seq_of(xh, z, y):
    return xh * 32 + z * 4 + y


def remote(src, dst, send, recv, device):
    return pltpu.make_async_remote_copy(
        src_ref=src, dst_ref=dst, send_sem=send, recv_sem=recv, device_id=device, device_id_type=MESH
    )


def greet(barrier, device):
    pl.semaphore_signal(barrier, inc=1, device_id=device, device_id_type=MESH)


def sigma_rows(step_ref):
    step = jnp.full((8, 128), step_ref[0], jnp.int32).astype(F32)
    frac = (step + 1.0) / NT
    return (SHIFT_VALUE * frac / (1.0 + (SHIFT_VALUE - 1.0) * frac))[0:1, :]


def split2(value):
    high = value.astype(BF16)
    low = (value - high.astype(F32)).astype(BF16)
    return high, low


def pack(value):
    return jnp.concatenate([value[:32], value[32:]], axis=1)


def vmem(n):
    return [pl.BlockSpec(memory_space=pltpu.VMEM)] * n


def features(x):
    return x + x * jnp.tanh(x * (GA + GB * (x * x)))


ORDER = (0, 1, 7, 2, 6, 3, 5, 4)
W_Y, W_C, U_Y, G_X, G_Z, E_Z, E_Y, K_C = 0, 2, 4, 5, 9, 16, 24, 28
A_Z, B_X, L_Z, L_Y, X_X, F_Z, F_Y, F_C, N_SEM = 34, 42, 50, 58, 82, 90, 98, 122, 126


def window_kernel(
    lat_ref, noise_ref, gs_ref, cs_ref, gin_ref, gout_ref, embed_ref, out_ref, weight_ref,
    dmd_out, grads_out,
    pre_s, mine_s, rows_s, w_s, acc, ssq, qq, kk, vv, uu, um, vel_s,
    eb, lb, arrive_a, part_b, arrive_b, n_s, slope_s, hid_s, piece_s, arrive_x, fin,
    send, recv, local,
):
    b, xh, z, y, c = place()
    j = y % 2
    y_high = y // 2
    is_self = jnp.logical_and(j == c, y_high == c)
    barrier = pltpu.get_barrier_semaphore()
    me = (b, seq_of(xh, z, y), c)
    sibling = (b, seq_of(xh, z, y), 1 - c)
    partner = (b, seq_of(xh, z, y + 1 - 2 * j), c)

    def at_z(d):
        return (b, seq_of(xh, (z + d) % 8, y), c)

    def at_y(d):
        return (b, seq_of(xh, z, (y + d) % 4), c)

    def at_x(k):
        return ((b + k // 4) % 2, seq_of((xh + k // 2 % 2) % 2, z, y), (c + k % 2) % 2)

    def source_g_self(k):
        return jnp.logical_and(is_self, jnp.logical_and(xh == k // 2, j == k % 2))

    def target_g_self(k):
        return jnp.logical_and(is_self, jnp.logical_and(xh == k // 2, y_high == k % 2))

    def source_b_self(k):
        return jnp.logical_and(target_g_self(k % 4), b == k // 4)

    def target_b_self(k):
        return jnp.logical_and(source_g_self(k % 4), b == k // 4)

    for k in range(4):
        @pl.when(jnp.logical_not(source_g_self(k)))
        def _():
            greet(barrier, (b, seq_of(k // 2, z, 2 * c + k % 2), j))

    for k in range(8):
        @pl.when(jnp.logical_not(source_b_self(k)))
        def _():
            greet(barrier, (k // 4, seq_of(k // 2 % 2, z, c + 2 * (k % 2)), y_high))

    for d in range(1, 8):
        greet(barrier, at_z(d))
        greet(barrier, at_x(d))
    for d in range(1, 4):
        greet(barrier, at_y(d))
    own_weight = pltpu.make_async_copy(weight_ref, w_s.at[pl.ds(0, 2)], local.at[0])
    own_weight.start()

    sg = sigma_rows(gs_ref)
    sc = sigma_rows(cs_ref)
    lat = lat_ref[...]
    um[0] = jnp.concatenate([out_ref[...], jnp.zeros((64, 64), BF16)], axis=1)
    squares = jnp.zeros((64, 128), F32)
    width = 512
    for t in range(D // width):
        cols = slice(t * width, (t + 1) * width)
        pre = dot(lat, gin_ref[:, cols])
        pre_s[:, cols] = pre
        sq = pre * pre
        for u in range(width // 128):
            squares = squares + sq[:, u * 128 : (u + 1) * 128]
    scale = lax.rsqrt(jnp.sum(squares, axis=-1, keepdims=True) / D + EPS_NORM)

    pl.semaphore_wait(barrier, 29 - 2 * is_self.astype(jnp.int32))

    def weight_copy(q):
        rows = pl.ds(q * PART, PART)
        return remote(
            weight_ref.at[c, rows], w_s.at[2, rows], send.at[W_Y + q], recv.at[W_Y + q], partner
        )

    def weight_forward(q):
        rows = pl.ds(q * PART, PART)
        return remote(w_s.at[2, rows], w_s.at[3, rows], send.at[W_C + q], recv.at[W_C + q], sibling)

    out_copy = remote(um.at[0], um.at[1], send.at[U_Y], recv.at[U_Y], partner)
    weight_copy(0).start()
    weight_copy(1).start()

    out = jnp.zeros((64, LAT), F32)
    for t in range(D // width):
        cols = slice(t * width, (t + 1) * width)
        n = pre_s[:, cols] * scale
        th = jnp.tanh(n * (GA + GB * (n * n)))
        out = out + dot_nt((0.5 * n * (1.0 + th)).astype(BF16), gout_ref[:, cols])
    lat_f = lat.astype(F32)
    clean = lat_f - sg[:, :64] * out
    noisy = ((1.0 - sc[:, :64]) * clean + sc[:, :64] * noise_ref[...].astype(F32)).astype(BF16)
    mine = pack(noisy)
    mine_s[...] = mine
    slot = xh * 2 + j

    @pl.when(is_self)
    def _():
        rows_s[0, slot] = mine

    def first(k):
        device = (b, seq_of(k // 2, z, c + 2 * (k % 2)), y_high)
        return remote(mine_s, rows_s.at[0, slot], send.at[G_X + k], recv.at[G_X + slot], device)

    for k in range(4):
        @pl.when(jnp.logical_not(target_g_self(k)))
        def _():
            first(k).start()

    clean = pack(clean)
    high, low = split2(lat_f * scale)
    early = jnp.concatenate([high, low], axis=1)
    eb[0, 0] = jnp.where(b == 0, early[:32], early[32:])

    for k in range(4):
        @pl.when(jnp.logical_not(source_g_self(k)))
        def _():
            remote(mine_s, rows_s.at[0, k], send.at[G_X + k], recv.at[G_X + k], me).wait_recv()

    def second(p):
        d = ORDER[p]
        return remote(
            rows_s.at[0], rows_s.at[p], send.at[G_Z + p - 1], recv.at[G_Z + p - 1], at_z(d)
        )

    for p in range(1, 8):
        second(p).start()

    def along_z(buf, base, d):
        return remote(buf.at[0, 0], buf.at[0, d], send.at[base + d], recv.at[base + d], at_z(d))

    def early_y(d):
        return remote(eb.at[0], eb.at[d], send.at[E_Y + d], recv.at[E_Y + d], at_y(d))

    def late_y(e, d):
        n = L_Y + (e - 1) * 8 + d
        return remote(lb.at[0, d], lb.at[e, d], send.at[n], recv.at[n], at_y(e))

    out_copy.start()
    for d in range(1, 8):
        along_z(eb, E_Z, d).start()

    qv = jnp.zeros((64, LAT), F32)
    for t in range(D // width):
        cols = slice(t * width, (t + 1) * width)
        n = pre_s[:, cols] * scale
        n2 = n * n
        th = jnp.tanh(n * (GA + GB * n2))
        slope = 0.5 * (1.0 + th) + 0.5 * n * (1.0 - th * th) * (GA + 3.0 * GB * n2)
        qv = qv + dot_nt((slope * n).astype(BF16), gout_ref[:, cols])
    my_q = jnp.where(b == 0, qv[:32], qv[32:])
    vv[:, HD:] = jnp.ones((2 * ROWS, HD), BF16)
    own_weight.wait()

    def key_copy(side, part):
        rows = pl.ds(side * 1024, 1024)
        there = pl.ds(ROWS + side * 1024, 1024)
        n = K_C + side * 3 + part
        if part == 2:
            return remote(vv.at[rows, pl.ds(0, HD)], vv.at[there, pl.ds(0, HD)], send.at[n], recv.at[n], sibling)
        return remote(
            kk.at[rows, pl.ds(0, HD)], kk.at[there, pl.ds(part * HD, HD)], send.at[n], recv.at[n], sibling
        )

    starts = (j * HALF, j * HALF + CHUNK, (1 - j) * HALF + c * CHUNK, (1 - j) * HALF + (1 - c) * CHUNK)
    for f in range(4):
        embed = embed_ref[:, pl.ds(pl.multiple_of(starts[f], 128), CHUNK)]
        if f == 1:
            weight_copy(0).wait_recv()
            weight_forward(0).start()
            for d in range(1, 8):
                along_z(eb, E_Z, d).wait_recv()
            for d in range(1, 4):
                early_y(d).start()
        if f == 2:
            weight_copy(1).wait_recv()
            weight_forward(1).start()
        if f == 3:
            weight_forward(0).wait_recv()
            weight_forward(1).wait_recv()

        def activate(t):
            side, part = t // 4, t % 4
            if f == 0 and side == 0:
                for p in (2 * part, 2 * part + 1):
                    if p > 0:
                        second(p).wait_recv()
            tile = rows_s[2 * part : 2 * part + 2].reshape(TILE, 128)
            x = dot(tile[:, side * 64 : (side + 1) * 64], embed)
            e = features(x)
            squares = e * e
            total = squares[:, :128]
            for u in range(1, CHUNK // 128):
                total = total + squares[:, u * 128 : (u + 1) * 128]
            rows = slice(t * TILE, (t + 1) * TILE)
            ssq[rows, :] = total if f == 0 else ssq[rows, :] + total
            return e.astype(BF16)

        def accumulate(t, e):
            rows = slice(t * TILE, (t + 1) * TILE)
            got = dot(e, w_s[f])
            if f > 0:
                got = got + acc[rows, :]
            if f < 3:
                acc[rows, :] = got
                return
            mean = jnp.sum(ssq[rows, :], axis=-1, keepdims=True) / D
            got = (got * lax.rsqrt(mean + 4.0 * EPS_NORM)).astype(BF16)
            qq[rows, :] = jnp.concatenate(split2(got[:, :HD].astype(F32) * SCORE_SCALE), axis=1)
            kk[rows, :] = jnp.concatenate([got[:, HD : 2 * HD]] * 2, axis=1)
            vv[rows, :HD] = got[:, 2 * HD :]
            if t % 4 == 3:
                for part in range(3):
                    key_copy(t // 4, part).start()

        before = activate(0)
        for t in range(1, 8):
            now = activate(t)
            accumulate(t - 1, before)
            before = now
        accumulate(7, before)

    out_copy.wait_recv()
    own = um[0][:, :64]
    other = um[1][:, :64]
    full = jnp.concatenate([jnp.where(j == 0, own, other), jnp.where(j == 0, other, own)], axis=0)
    none = jnp.zeros((HD, LAT), BF16)
    uu[:HD, :] = jnp.concatenate([full, none], axis=1)
    uu[HD:, :] = jnp.concatenate([none, full], axis=1)
    for side in range(2):
        for part in range(3):
            key_copy(side, part).wait_recv()

    def vel_copy(p):
        e = (8 - ORDER[p]) % 8
        return remote(vel_s.at[p], arrive_a.at[e - 1], send.at[A_Z + e], recv.at[A_Z + e], at_z(e))

    def scores(p):
        query = jnp.concatenate(
            [qq[p * 128 : (p + 1) * 128, :], qq[1024 + p * 128 : 1024 + (p + 1) * 128, :]], axis=0
        )
        return dot_nt(query, kk[...])

    def mix(s):
        top = jnp.max(s, axis=-1, keepdims=True)
        got = dot(jnp.exp2(s - top).astype(BF16), vv[...])
        attended = (got[:, :HD] / got[:, HD:]).astype(BF16)
        return jnp.concatenate([attended[:128], attended[128:]], axis=1)

    def velocity(p, both):
        vel_s[p] = dot(both, uu[...]).astype(BF16)
        if p > 0:
            vel_copy(p).start()

    s_next = scores(7)
    both = None
    for p in range(7, -1, -1):
        s_now = s_next
        if p > 0:
            s_next = scores(p - 1)
        if both is not None:
            velocity(p + 1, both)
        both = mix(s_now)
    velocity(0, both)

    start = (y * 8 + z) * 160
    window = pl.ds(pl.multiple_of(start // 128 * 128, 128), 256)
    row = lax.broadcasted_iota(jnp.int32, (160, 256), 0)
    col = lax.broadcasted_iota(jnp.int32, (160, 256), 1)
    choose = jnp.where(col == row + start % 128, 1.0, 0.0).astype(BF16)
    cut = gin_ref[:, window]
    gi = dot_nt(choose, jnp.concatenate([cut, cut], axis=0)).astype(BF16)
    cut = gout_ref[:, window]
    go = dot_nt(choose, jnp.concatenate([cut, jnp.zeros_like(cut)], axis=0)).astype(BF16)

    total = vel_s[0].astype(F32)
    for p in range(7, 0, -1):
        vel_copy(p).wait_recv()
        total = total + arrive_a[(8 - ORDER[p]) % 8 - 1].astype(F32)
    for k in range(4):
        part_b[k] = total[k * 32 : (k + 1) * 32]
    slot_b = b * 4 + xh * 2 + y_high

    def part_copy(k):
        device = (k // 4, seq_of(k // 2 % 2, z, 2 * c + k % 2), j)
        return remote(part_b.at[k % 4], arrive_b.at[slot_b], send.at[B_X + k], recv.at[B_X + slot_b], device)

    for k in range(8):
        @pl.when(jnp.logical_not(target_b_self(k)))
        def _():
            part_copy(k).start()

        @pl.when(target_b_self(k))
        def _():
            arrive_b[slot_b] = part_b[k % 4]

    for d in range(1, 4):
        early_y(d).wait_recv()
    early = eb[...].reshape(1024, 128)
    n = dot_nt(gi, early)
    n2 = n * n
    th = jnp.tanh(n * (GA + GB * n2))
    n_s[...] = n
    hid_s[...] = (0.5 * n * (1.0 + th)).astype(BF16)
    slope_s[...] = 0.5 * (1.0 + th) + 0.5 * n * (1.0 - th * th) * (GA + 3.0 * GB * n2)

    for k in range(8):
        @pl.when(jnp.logical_not(source_b_self(k)))
        def _():
            remote(
                part_b.at[k % 4], arrive_b.at[k], send.at[B_X + k], recv.at[B_X + k], me
            ).wait_recv()

    teacher = arrive_b[0] + arrive_b[1] + arrive_b[2] + arrive_b[3]
    fake = arrive_b[4] + arrive_b[5] + arrive_b[6] + arrive_b[7]
    gap = fake - teacher
    away = jnp.abs(clean - (mine_s[...].astype(F32) - sc * teacher))
    my_gap = jnp.where(b == 0, gap[:, :64], gap[:, 64:])
    my_away = jnp.where(b == 0, away[:, :64], away[:, 64:])
    away_row = jnp.sum(my_away, axis=-1, keepdims=True)
    rbar = jnp.sum(my_gap * my_q, axis=-1, keepdims=True) / D
    r_high, r_low = split2(rbar)
    a_high, a_low = split2(away_row)
    a_rest = (away_row - a_high.astype(F32) - a_low.astype(F32)).astype(BF16)
    lane = lax.broadcasted_iota(jnp.int32, (32, 64), 1)
    extra = jnp.zeros((32, 64), F32)
    for at, value in enumerate((r_high, r_low, a_high, a_low, a_rest)):
        extra = jnp.where(lane == at, value.astype(F32), extra)
    lb[0, 0] = jnp.concatenate([my_gap, extra], axis=1).astype(BF16)

    for d in range(1, 8):
        along_z(lb, L_Z, d).start()
    for e in range(1, 4):
        late_y(e, 0).start()
    for d in ORDER[1:]:
        along_z(lb, L_Z, d).wait_recv()
        for e in range(1, 4):
            late_y(e, d).start()
    for d in range(8):
        for e in range(1, 4):
            late_y(e, d).wait_recv()
    late = lb[...].reshape(1024, 128)
    lane = lax.broadcasted_iota(jnp.int32, (16, 128), 1)
    pick = jnp.where(jnp.logical_or(lane == 64, lane == 65), 1.0, 0.0).astype(BF16)
    rbar_all = dot_nt(pick, late)[0:1, :]
    away_all = dot(jnp.ones((16, 1024), BF16), late)[0:1, :]
    lane1 = lax.broadcasted_iota(jnp.int32, (1, 128), 1)
    away_sum = jnp.sum(
        jnp.where(jnp.logical_and(lane1 >= 66, lane1 <= 68), away_all, 0.0), axis=-1, keepdims=True
    )
    dpre = (slope_s[...] * dot_nt(go, late) - n_s[...] * rbar_all).astype(BF16)
    grad_in = dot(dpre, early)
    grad_out = dot(hid_s[...], late)
    piece = jnp.concatenate([grad_in[:, :64] + grad_in[:, 64:], grad_out[:, :64]], axis=1)
    row8 = lax.broadcasted_iota(jnp.int32, (8, 128), 0)
    extra8 = jnp.where(row8 == 0, away_sum, sg * sc)
    for p in range(2):
        piece_s[p, :80] = piece[p * 80 : (p + 1) * 80]
        piece_s[p, 80:] = extra8

    def piece_copy(k):
        return remote(
            piece_s.at[(c + k % 2) % 2], arrive_x.at[k], send.at[X_X + k], recv.at[X_X + k], at_x(k)
        )

    for k in range(1, 8):
        piece_copy(k).start()
    arrive_x[0] = piece_s[c]
    for k in range(1, 8):
        piece_copy(k).wait_recv()
    same = arrive_x[0] + arrive_x[2] + arrive_x[4] + arrive_x[6]
    cross = arrive_x[1] + arrive_x[3] + arrive_x[5] + arrive_x[7]
    spread = same[80:81] / COUNT + EPS_SPREAD
    spread_cross = cross[80:81] / COUNT + EPS_SPREAD
    result = (0.25 * same[81:82] / spread) * same[:80] + (0.25 * cross[81:82] / spread_cross) * cross[:80]
    fin[y, z, c] = result.astype(BF16)

    def out_z(d):
        at = fin.at[y, z, c]
        return remote(at, at, send.at[F_Z + d], recv.at[F_Z + d], at_z(d))

    def out_z_here(d):
        at = fin.at[y, (z + 8 - d) % 8, c]
        return remote(at, at, send.at[F_Z + d], recv.at[F_Z + d], at_z(d))

    def out_y(e, d):
        n = F_Y + (e - 1) * 8 + d
        at = fin.at[y, (z + 8 - d) % 8, c]
        return remote(at, at, send.at[n], recv.at[n], at_y(e))

    def out_y_here(e, d):
        n = F_Y + (e - 1) * 8 + d
        at = fin.at[(y + 4 - e) % 4, (z + 8 - d) % 8, c]
        return remote(at, at, send.at[n], recv.at[n], at_y(e))

    def out_core(e):
        at = fin.at[(y + 4 - e) % 4, :, c]
        return remote(at, at, send.at[F_C + e], recv.at[F_C + e], sibling)

    def out_core_here(e):
        at = fin.at[(y + 4 - e) % 4, :, 1 - c]
        return remote(at, at, send.at[F_C + e], recv.at[F_C + e], sibling)

    for d in range(1, 8):
        out_z(d).start()
    for e in range(1, 4):
        out_y(e, 0).start()
    dmd_out[...] = -sc * gap / spread
    for d in ORDER[1:]:
        out_z_here(d).wait_recv()
        for e in range(1, 4):
            out_y(e, d).start()
    out_core(0).start()
    for e in (1, 3, 2):
        for d in range(8):
            out_y_here(e, d).wait_recv()
        out_core(e).start()
    for e in range(4):
        out_core_here(e).wait_recv()
    grads_out[...] = fin[...]

    for k in range(4):
        @pl.when(jnp.logical_not(target_g_self(k)))
        def _():
            first(k).wait_send()
    for k in range(8):
        @pl.when(jnp.logical_not(target_b_self(k)))
        def _():
            part_copy(k).wait_send()
    for q in range(2):
        weight_copy(q).wait_send()
        weight_forward(q).wait_send()
        for part in range(3):
            key_copy(q, part).wait_send()
    out_copy.wait_send()
    for d in range(1, 8):
        second(d).wait_send()
        along_z(eb, E_Z, d).wait_send()
        vel_copy(d).wait_send()
        along_z(lb, L_Z, d).wait_send()
        piece_copy(d).wait_send()
        out_z(d).wait_send()
    for e in range(1, 4):
        early_y(e).wait_send()
        for d in range(8):
            late_y(e, d).wait_send()
            out_y(e, d).wait_send()
    for e in range(4):
        out_core(e).wait_send()


def window(latent, noise, gen_step, critic_step, gen_in, gen_out_t, embed, out, weight):
    smem = pl.BlockSpec(memory_space=pltpu.SMEM)
    return pl.pallas_call(
        window_kernel,
        out_shape=(
            jax.ShapeDtypeStruct((32, 128), F32),
            jax.ShapeDtypeStruct((4, 8, 2, 80, 128), BF16),
        ),
        in_specs=vmem(2) + [smem, smem] + vmem(4) + [pl.BlockSpec(memory_space=pl.ANY)],
        out_specs=tuple(vmem(2)),
        scratch_shapes=[
            pltpu.VMEM((64, D), F32),
            pltpu.VMEM((32, 128), BF16),
            pltpu.VMEM((8, 4, 32, 128), BF16),
            pltpu.VMEM((4, CHUNK, 3 * HD), BF16),
            pltpu.VMEM((ROWS, 3 * HD), F32),
            pltpu.VMEM((ROWS, 128), F32),
            pltpu.VMEM((ROWS, 2 * HD), BF16),
            pltpu.VMEM((2 * ROWS, 2 * HD), BF16),
            pltpu.VMEM((2 * ROWS, 2 * HD), BF16),
            pltpu.VMEM((2 * HD, 128), BF16),
            pltpu.VMEM((2, 64, 128), BF16),
            pltpu.VMEM((8, 128, 128), BF16),
            pltpu.VMEM((4, 8, 32, 128), BF16),
            pltpu.VMEM((4, 8, 32, 128), BF16),
            pltpu.VMEM((7, 128, 128), BF16),
            pltpu.VMEM((4, 32, 128), F32),
            pltpu.VMEM((8, 32, 128), F32),
            pltpu.VMEM((160, 1024), F32),
            pltpu.VMEM((160, 1024), F32),
            pltpu.VMEM((160, 1024), BF16),
            pltpu.VMEM((2, 88, 128), F32),
            pltpu.VMEM((8, 88, 128), F32),
            pltpu.VMEM((4, 8, 2, 80, 128), BF16),
            pltpu.SemaphoreType.DMA((N_SEM,)),
            pltpu.SemaphoreType.DMA((N_SEM,)),
            pltpu.SemaphoreType.DMA((1,)),
        ],
        compiler_params=pltpu.CompilerParams(
            collective_id=0, has_side_effects=True, vmem_limit_bytes=56 << 20
        ),
    )(latent, noise, gen_step, critic_step, gen_in, gen_out_t, embed, out, weight)


def unpack_kernel(dmd_ref, grads_ref, dmd_out, in_out, out_out):
    dmd_out[:32] = dmd_ref[:, :64]
    dmd_out[32:] = dmd_ref[:, 64:]
    row = lax.broadcasted_iota(jnp.int32, (128, 128), 0)
    col = lax.broadcasted_iota(jnp.int32, (128, 128), 1)
    same = jnp.where(row == col, 1.0, 0.0).astype(BF16)
    width = 1280
    for t in range(D // width):
        cols = slice(t * width, (t + 1) * width)
        turned = dot_nt(same, grads_ref[cols, :])
        in_out[:, cols] = turned[:64]
        out_out[:, cols] = turned[64:]


def unpack(dmd, grads):
    return pl.pallas_call(
        unpack_kernel,
        out_shape=(
            jax.ShapeDtypeStruct((64, 64), F32),
            jax.ShapeDtypeStruct((64, D), F32),
            jax.ShapeDtypeStruct((64, D), F32),
        ),
        in_specs=vmem(2),
        out_specs=tuple(vmem(3)),
        compiler_params=pltpu.CompilerParams(vmem_limit_bytes=24 << 20),
    )(dmd, grads)


def per_device(
    gen_input, noise, gen_step, critic_step, gen_in, gen_out, critic_embed, critic_qkv, critic_out
):
    weight = critic_qkv.reshape(2, CHUNK, 3 * HD)
    dmd, grads = window(
        gen_input[0], noise[0], gen_step, critic_step, gen_in, gen_out.T, critic_embed[0],
        critic_out[0, 0], weight,
    )
    dmd, grad_in, grad_out = unpack(dmd, grads.reshape(D, 128))
    return (dmd[None], grad_in, grad_out.T)


def solution(mesh):
    return jax.shard_map(
        per_device,
        mesh=mesh,
        in_specs=(
            P("dp", "seq", None),
            P("dp", "seq", None),
            P("dp"),
            P("dp"),
            P(),
            P(),
            P("grp", None, None),
            P("grp", "seq", None, None),
            P("grp", "seq", None, None),
        ),
        out_specs=(P("dp", "seq", None), P(), P()),
        check_vma=False,
    )
```

```python
import jax
import jax.numpy as jnp
from jax import lax
from jax.experimental import pallas as pl
from jax.experimental.pallas import tpu as pltpu
from jax.sharding import PartitionSpec as P

F32 = jnp.float32
BF16 = jnp.bfloat16
NT = 1000
D = 5120
HALF = 2560
LAT = 64
HD = 128
ROWS = 2048
TILE = 256
PART = 320
CHUNK = 1280
SHIFT_VALUE = 5.0
EPS_NORM = 1e-06
EPS_SPREAD = 1e-06
COUNT = 4096 * 64
GA = 0.7978845608028654
GB = GA * 0.044715
SCORE_SCALE = 1.4426950408889634 * HD**-0.5
MESH = pl.DeviceIdType.MESH
CONTRACT_LAST = (((1,), (1,)), ((), ()))


def dot(a, b):
    return jnp.dot(a, b, preferred_element_type=F32)


def dot_nt(a, b):
    return lax.dot_general(a, b, CONTRACT_LAST, preferred_element_type=F32)


def place():
    b = lax.axis_index("grp")
    s = lax.axis_index("seq")
    c = lax.axis_index("dp")
    return b, s // 32, (s // 4) % 8, s % 4, c


def seq_of(xh, z, y):
    return xh * 32 + z * 4 + y


def remote(src, dst, send, recv, device):
    return pltpu.make_async_remote_copy(
        src_ref=src, dst_ref=dst, send_sem=send, recv_sem=recv, device_id=device, device_id_type=MESH
    )


def greet(barrier, device):
    pl.semaphore_signal(barrier, inc=1, device_id=device, device_id_type=MESH)


def sigma_rows(step_ref):
    step = jnp.full((8, 128), step_ref[0], jnp.int32).astype(F32)
    frac = (step + 1.0) / NT
    return (SHIFT_VALUE * frac / (1.0 + (SHIFT_VALUE - 1.0) * frac))[0:1, :]


def split2(value):
    high = value.astype(BF16)
    low = (value - high.astype(F32)).astype(BF16)
    return high, low


def pack(value):
    return jnp.concatenate([value[:32], value[32:]], axis=1)


def vmem(n):
    return [pl.BlockSpec(memory_space=pltpu.VMEM)] * n


def features(x):
    return x + x * jnp.tanh(x * (GA + GB * (x * x)))


ORDER = (0, 1, 7, 2, 6, 3, 5, 4)
W_Y, W_C, U_Y, G_X, G_Z, E_Z, E_Y, K_C = 0, 126, 4, 5, 9, 16, 24, 28
A_Z, B_X, L_Z, L_Y, X_X, F_Z, F_Y, F_C, N_SEM = 34, 42, 50, 58, 82, 90, 98, 122, 130


def window_kernel(
    lat_ref, noise_ref, gs_ref, cs_ref, gin_ref, gout_ref, embed_ref, out_ref, weight_ref,
    dmd_out, grads_out,
    pre_s, mine_s, rows_s, w_s, acc, ssq, qq, kk, vv, uu, um, vel_s,
    eb, lb, arrive_a, part_b, arrive_b, n_s, slope_s, hid_s, piece_s, arrive_x, fin,
    q_s, gi_s, go_s, send, recv, local,
):
    b, xh, z, y, c = place()
    j = y % 2
    y_high = y // 2
    is_self = jnp.logical_and(j == c, y_high == c)
    barrier = pltpu.get_barrier_semaphore()
    me = (b, seq_of(xh, z, y), c)
    sibling = (b, seq_of(xh, z, y), 1 - c)
    partner = (b, seq_of(xh, z, y + 1 - 2 * j), c)

    def at_z(d):
        return (b, seq_of(xh, (z + d) % 8, y), c)

    def at_y(d):
        return (b, seq_of(xh, z, (y + d) % 4), c)

    def at_x(k):
        return ((b + k // 4) % 2, seq_of((xh + k // 2 % 2) % 2, z, y), (c + k % 2) % 2)

    def source_g_self(k):
        return jnp.logical_and(is_self, jnp.logical_and(xh == k // 2, j == k % 2))

    def target_g_self(k):
        return jnp.logical_and(is_self, jnp.logical_and(xh == k // 2, y_high == k % 2))

    def source_b_self(k):
        return jnp.logical_and(target_g_self(k % 4), b == k // 4)

    def target_b_self(k):
        return jnp.logical_and(source_g_self(k % 4), b == k // 4)

    for k in range(4):
        @pl.when(jnp.logical_not(source_g_self(k)))
        def _():
            greet(barrier, (b, seq_of(k // 2, z, 2 * c + k % 2), j))

    for k in range(8):
        @pl.when(jnp.logical_not(source_b_self(k)))
        def _():
            greet(barrier, (k // 4, seq_of(k // 2 % 2, z, c + 2 * (k % 2)), y_high))

    for d in range(1, 8):
        greet(barrier, at_z(d))
        greet(barrier, at_x(d))
    for d in range(1, 4):
        greet(barrier, at_y(d))
    own_weight = pltpu.make_async_copy(weight_ref, w_s.at[pl.ds(0, 2)], local.at[0])
    own_weight.start()

    sg = sigma_rows(gs_ref)
    sc = sigma_rows(cs_ref)
    lat = lat_ref[...]
    um[0] = jnp.concatenate([out_ref[...], jnp.zeros((64, 64), BF16)], axis=1)
    squares = jnp.zeros((64, 128), F32)
    width = 512
    for t in range(D // width):
        cols = slice(t * width, (t + 1) * width)
        pre = dot(lat, gin_ref[:, cols])
        pre_s[:, cols] = pre
        sq = pre * pre
        for u in range(width // 128):
            squares = squares + sq[:, u * 128 : (u + 1) * 128]
    scale = lax.rsqrt(jnp.sum(squares, axis=-1, keepdims=True) / D + EPS_NORM)

    def weight_copy(q):
        rows = pl.ds(q * PART, PART)
        return remote(
            weight_ref.at[c, rows], w_s.at[2, rows], send.at[W_Y + q], recv.at[W_Y + q], partner
        )

    def weight_forward(q):
        rows = pl.ds(q * PART, PART)
        return remote(w_s.at[2, rows], w_s.at[3, rows], send.at[W_C + q], recv.at[W_C + q], sibling)

    out_copy = remote(um.at[0], um.at[1], send.at[U_Y], recv.at[U_Y], partner)

    out = jnp.zeros((64, LAT), F32)
    for t in range(D // width):
        cols = slice(t * width, (t + 1) * width)
        n = pre_s[:, cols] * scale
        th = jnp.tanh(n * (GA + GB * (n * n)))
        out = out + dot_nt((0.5 * n * (1.0 + th)).astype(BF16), gout_ref[:, cols])
    lat_f = lat.astype(F32)
    clean = lat_f - sg[:, :64] * out
    noisy = ((1.0 - sc[:, :64]) * clean + sc[:, :64] * noise_ref[...].astype(F32)).astype(BF16)
    mine = pack(noisy)
    mine_s[...] = mine
    slot = xh * 2 + j

    @pl.when(is_self)
    def _():
        rows_s[0, slot] = mine

    pl.semaphore_wait(barrier, 29 - 2 * is_self.astype(jnp.int32))

    def first(k):
        device = (b, seq_of(k // 2, z, c + 2 * (k % 2)), y_high)
        return remote(mine_s, rows_s.at[0, slot], send.at[G_X + k], recv.at[G_X + slot], device)

    for k in range(4):
        @pl.when(jnp.logical_not(target_g_self(k)))
        def _():
            first(k).start()

    clean = pack(clean)
    high, low = split2(lat_f * scale)
    early = jnp.concatenate([high, low], axis=1)
    eb[0, 0] = jnp.where(b == 0, early[:32], early[32:])

    for k in range(4):
        @pl.when(jnp.logical_not(source_g_self(k)))
        def _():
            remote(mine_s, rows_s.at[0, k], send.at[G_X + k], recv.at[G_X + k], me).wait_recv()

    def second(p):
        d = ORDER[p]
        return remote(
            rows_s.at[0], rows_s.at[p], send.at[G_Z + p - 1], recv.at[G_Z + p - 1], at_z(d)
        )

    for p in range(1, 8):
        second(p).start()

    def along_z(buf, base, d):
        return remote(buf.at[0, 0], buf.at[0, d], send.at[base + d], recv.at[base + d], at_z(d))

    def early_y(d):
        return remote(eb.at[0], eb.at[d], send.at[E_Y + d], recv.at[E_Y + d], at_y(d))

    def late_y(e, d):
        n = L_Y + (e - 1) * 8 + d
        return remote(lb.at[0, d], lb.at[e, d], send.at[n], recv.at[n], at_y(e))

    out_copy.start()
    for d in range(1, 8):
        along_z(eb, E_Z, d).start()
    for q in range(4):
        weight_copy(q).start()

    vv[:, HD:] = jnp.ones((2 * ROWS, HD), BF16)
    own_weight.wait()

    def key_copy(side, part):
        rows = pl.ds(side * 1024, 1024)
        there = pl.ds(ROWS + side * 1024, 1024)
        n = K_C + side * 3 + part
        if part == 2:
            return remote(vv.at[rows, pl.ds(0, HD)], vv.at[there, pl.ds(0, HD)], send.at[n], recv.at[n], sibling)
        return remote(
            kk.at[rows, pl.ds(0, HD)], kk.at[there, pl.ds(part * HD, HD)], send.at[n], recv.at[n], sibling
        )

    starts = (j * HALF, j * HALF + CHUNK, (1 - j) * HALF + c * CHUNK, (1 - j) * HALF + (1 - c) * CHUNK)
    for f in range(4):
        embed = embed_ref[:, pl.ds(pl.multiple_of(starts[f], 128), CHUNK)]
        if f == 1:
            for q in range(2):
                weight_copy(q).wait_recv()
                weight_forward(q).start()
            for d in range(1, 8):
                along_z(eb, E_Z, d).wait_recv()
            for d in range(1, 4):
                early_y(d).start()
        if f == 2:
            qv = jnp.zeros((64, LAT), F32)
            for t in range(D // width):
                cols = slice(t * width, (t + 1) * width)
                n = pre_s[:, cols] * scale
                n2 = n * n
                th = jnp.tanh(n * (GA + GB * n2))
                slope = 0.5 * (1.0 + th) + 0.5 * n * (1.0 - th * th) * (GA + 3.0 * GB * n2)
                qv = qv + dot_nt((slope * n).astype(BF16), gout_ref[:, cols])
            q_s[...] = jnp.where(b == 0, qv[:32], qv[32:])

            start = (y * 8 + z) * 160
            window = pl.ds(pl.multiple_of(start // 128 * 128, 128), 256)
            row = lax.broadcasted_iota(jnp.int32, (160, 256), 0)
            col = lax.broadcasted_iota(jnp.int32, (160, 256), 1)
            choose = jnp.where(col == row + start % 128, 1.0, 0.0).astype(BF16)
            cut = gin_ref[:, window]
            gi_s[...] = dot_nt(choose, jnp.concatenate([cut, cut], axis=0)).astype(BF16)
            cut = gout_ref[:, window]
            go_s[...] = dot_nt(choose, jnp.concatenate([cut, jnp.zeros_like(cut)], axis=0)).astype(BF16)

            for q in range(2, 4):
                weight_copy(q).wait_recv()
                weight_forward(q).start()
        if f == 3:
            for q in range(4):
                weight_forward(q).wait_recv()

        def activate(t):
            side, part = t // 4, t % 4
            if f == 0 and side == 0:
                for p in (2 * part, 2 * part + 1):
                    if p > 0:
                        second(p).wait_recv()
            tile = rows_s[2 * part : 2 * part + 2].reshape(TILE, 128)
            x = dot(tile[:, side * 64 : (side + 1) * 64], embed)
            e = features(x)
            squares = e * e
            total = squares[:, :128]
            for u in range(1, CHUNK // 128):
                total = total + squares[:, u * 128 : (u + 1) * 128]
            rows = slice(t * TILE, (t + 1) * TILE)
            ssq[rows, :] = total if f == 0 else ssq[rows, :] + total
            return e.astype(BF16)

        def accumulate(t, e):
            rows = slice(t * TILE, (t + 1) * TILE)
            got = dot(e, w_s[f])
            if f > 0:
                got = got + acc[rows, :]
            if f < 3:
                acc[rows, :] = got
                return
            mean = jnp.sum(ssq[rows, :], axis=-1, keepdims=True) / D
            got = (got * lax.rsqrt(mean + 4.0 * EPS_NORM)).astype(BF16)
            qq[rows, :] = jnp.concatenate(split2(got[:, :HD].astype(F32) * SCORE_SCALE), axis=1)
            kk[rows, :] = jnp.concatenate([got[:, HD : 2 * HD]] * 2, axis=1)
            vv[rows, :HD] = got[:, 2 * HD :]
            if t % 4 == 3:
                for part in range(3):
                    key_copy(t // 4, part).start()

        before = activate(0)
        for t in range(1, 8):
            now = activate(t)
            accumulate(t - 1, before)
            before = now
        accumulate(7, before)

    out_copy.wait_recv()
    own = um[0][:, :64]
    other = um[1][:, :64]
    full = jnp.concatenate([jnp.where(j == 0, own, other), jnp.where(j == 0, other, own)], axis=0)
    none = jnp.zeros((HD, LAT), BF16)
    uu[:HD, :] = jnp.concatenate([full, none], axis=1)
    uu[HD:, :] = jnp.concatenate([none, full], axis=1)
    for side in range(2):
        for part in range(3):
            key_copy(side, part).wait_recv()

    def vel_copy(p):
        e = (8 - ORDER[p]) % 8
        return remote(vel_s.at[p], arrive_a.at[e - 1], send.at[A_Z + e], recv.at[A_Z + e], at_z(e))

    def scores(p):
        query = jnp.concatenate(
            [qq[p * 128 : (p + 1) * 128, :], qq[1024 + p * 128 : 1024 + (p + 1) * 128, :]], axis=0
        )
        return dot_nt(query, kk[...])

    def mix(s):
        top = jnp.max(s, axis=-1, keepdims=True)
        got = dot(jnp.exp2(s - top).astype(BF16), vv[...])
        attended = (got[:, :HD] / got[:, HD:]).astype(BF16)
        return jnp.concatenate([attended[:128], attended[128:]], axis=1)

    def velocity(p, both):
        vel_s[p] = dot(both, uu[...]).astype(BF16)
        if p > 0:
            vel_copy(p).start()

    s_next = scores(7)
    both = None
    for p in range(7, -1, -1):
        s_now = s_next
        if p > 0:
            s_next = scores(p - 1)
        if both is not None:
            velocity(p + 1, both)
        both = mix(s_now)
    velocity(0, both)

    total = vel_s[0].astype(F32)
    for p in range(7, 0, -1):
        vel_copy(p).wait_recv()
        total = total + arrive_a[(8 - ORDER[p]) % 8 - 1].astype(F32)
    for k in range(4):
        part_b[k] = total[k * 32 : (k + 1) * 32]
    slot_b = b * 4 + xh * 2 + y_high

    def part_copy(k):
        device = (k // 4, seq_of(k // 2 % 2, z, 2 * c + k % 2), j)
        return remote(part_b.at[k % 4], arrive_b.at[slot_b], send.at[B_X + k], recv.at[B_X + slot_b], device)

    for k in range(8):
        @pl.when(jnp.logical_not(target_b_self(k)))
        def _():
            part_copy(k).start()

        @pl.when(target_b_self(k))
        def _():
            arrive_b[slot_b] = part_b[k % 4]

    for d in range(1, 4):
        early_y(d).wait_recv()
    early = eb[...].reshape(1024, 128)
    n = dot_nt(gi_s[...], early)
    n2 = n * n
    th = jnp.tanh(n * (GA + GB * n2))
    n_s[...] = n
    hid_s[...] = (0.5 * n * (1.0 + th)).astype(BF16)
    slope_s[...] = 0.5 * (1.0 + th) + 0.5 * n * (1.0 - th * th) * (GA + 3.0 * GB * n2)

    for k in range(8):
        @pl.when(jnp.logical_not(source_b_self(k)))
        def _():
            remote(
                part_b.at[k % 4], arrive_b.at[k], send.at[B_X + k], recv.at[B_X + k], me
            ).wait_recv()

    teacher = arrive_b[0] + arrive_b[1] + arrive_b[2] + arrive_b[3]
    fake = arrive_b[4] + arrive_b[5] + arrive_b[6] + arrive_b[7]
    gap = fake - teacher
    away = jnp.abs(clean - (mine_s[...].astype(F32) - sc * teacher))
    my_gap = jnp.where(b == 0, gap[:, :64], gap[:, 64:])
    my_away = jnp.where(b == 0, away[:, :64], away[:, 64:])
    away_row = jnp.sum(my_away, axis=-1, keepdims=True)
    rbar = jnp.sum(my_gap * q_s[...], axis=-1, keepdims=True) / D
    r_high, r_low = split2(rbar)
    a_high, a_low = split2(away_row)
    a_rest = (away_row - a_high.astype(F32) - a_low.astype(F32)).astype(BF16)
    lane = lax.broadcasted_iota(jnp.int32, (32, 64), 1)
    extra = jnp.zeros((32, 64), F32)
    for at, value in enumerate((r_high, r_low, a_high, a_low, a_rest)):
        extra = jnp.where(lane == at, value.astype(F32), extra)
    lb[0, 0] = jnp.concatenate([my_gap, extra], axis=1).astype(BF16)

    for d in range(1, 8):
        along_z(lb, L_Z, d).start()
    for e in range(1, 4):
        late_y(e, 0).start()
    for d in ORDER[1:]:
        along_z(lb, L_Z, d).wait_recv()
        for e in range(1, 4):
            late_y(e, d).start()
    for d in range(8):
        for e in range(1, 4):
            late_y(e, d).wait_recv()
    late = lb[...].reshape(1024, 128)
    lane = lax.broadcasted_iota(jnp.int32, (16, 128), 1)
    pick = jnp.where(jnp.logical_or(lane == 64, lane == 65), 1.0, 0.0).astype(BF16)
    rbar_all = dot_nt(pick, late)[0:1, :]
    away_all = dot(jnp.ones((16, 1024), BF16), late)[0:1, :]
    lane1 = lax.broadcasted_iota(jnp.int32, (1, 128), 1)
    away_sum = jnp.sum(
        jnp.where(jnp.logical_and(lane1 >= 66, lane1 <= 68), away_all, 0.0), axis=-1, keepdims=True
    )
    dpre = (slope_s[...] * dot_nt(go_s[...], late) - n_s[...] * rbar_all).astype(BF16)
    grad_in = dot(dpre, early)
    grad_out = dot(hid_s[...], late)
    piece = jnp.concatenate([grad_in[:, :64] + grad_in[:, 64:], grad_out[:, :64]], axis=1)
    row8 = lax.broadcasted_iota(jnp.int32, (8, 128), 0)
    extra8 = jnp.where(row8 == 0, away_sum, sg * sc)
    for p in range(2):
        piece_s[p, :80] = piece[p * 80 : (p + 1) * 80]
        piece_s[p, 80:] = extra8

    def piece_copy(k):
        return remote(
            piece_s.at[(c + k % 2) % 2], arrive_x.at[k], send.at[X_X + k], recv.at[X_X + k], at_x(k)
        )

    for k in range(1, 8):
        piece_copy(k).start()
    arrive_x[0] = piece_s[c]
    for k in range(1, 8):
        piece_copy(k).wait_recv()
    same = arrive_x[0] + arrive_x[2] + arrive_x[4] + arrive_x[6]
    cross = arrive_x[1] + arrive_x[3] + arrive_x[5] + arrive_x[7]
    spread = same[80:81] / COUNT + EPS_SPREAD
    spread_cross = cross[80:81] / COUNT + EPS_SPREAD
    result = (0.25 * same[81:82] / spread) * same[:80] + (0.25 * cross[81:82] / spread_cross) * cross[:80]
    fin[y, z, c] = result.astype(BF16)

    def out_z(d):
        at = fin.at[y, z, c]
        return remote(at, at, send.at[F_Z + d], recv.at[F_Z + d], at_z(d))

    def out_z_here(d):
        at = fin.at[y, (z + 8 - d) % 8, c]
        return remote(at, at, send.at[F_Z + d], recv.at[F_Z + d], at_z(d))

    def out_y(e, d):
        n = F_Y + (e - 1) * 8 + d
        at = fin.at[y, (z + 8 - d) % 8, c]
        return remote(at, at, send.at[n], recv.at[n], at_y(e))

    def out_y_here(e, d):
        n = F_Y + (e - 1) * 8 + d
        at = fin.at[(y + 4 - e) % 4, (z + 8 - d) % 8, c]
        return remote(at, at, send.at[n], recv.at[n], at_y(e))

    def out_core(e):
        at = fin.at[(y + 4 - e) % 4, :, c]
        return remote(at, at, send.at[F_C + e], recv.at[F_C + e], sibling)

    def out_core_here(e):
        at = fin.at[(y + 4 - e) % 4, :, 1 - c]
        return remote(at, at, send.at[F_C + e], recv.at[F_C + e], sibling)

    for d in range(1, 8):
        out_z(d).start()
    for e in range(1, 4):
        out_y(e, 0).start()
    dmd_out[...] = -sc * gap / spread
    for d in ORDER[1:]:
        out_z_here(d).wait_recv()
        for e in range(1, 4):
            out_y(e, d).start()
    out_core(0).start()
    for e in (1, 3, 2):
        for d in range(8):
            out_y_here(e, d).wait_recv()
        out_core(e).start()
    for e in range(4):
        out_core_here(e).wait_recv()
    grads_out[...] = fin[...]

    for k in range(4):
        @pl.when(jnp.logical_not(target_g_self(k)))
        def _():
            first(k).wait_send()
    for k in range(8):
        @pl.when(jnp.logical_not(target_b_self(k)))
        def _():
            part_copy(k).wait_send()
    for q in range(4):
        weight_copy(q).wait_send()
        weight_forward(q).wait_send()
    for side in range(2):
        for part in range(3):
            key_copy(side, part).wait_send()
    out_copy.wait_send()
    for d in range(1, 8):
        second(d).wait_send()
        along_z(eb, E_Z, d).wait_send()
        vel_copy(d).wait_send()
        along_z(lb, L_Z, d).wait_send()
        piece_copy(d).wait_send()
        out_z(d).wait_send()
    for e in range(1, 4):
        early_y(e).wait_send()
        for d in range(8):
            late_y(e, d).wait_send()
            out_y(e, d).wait_send()
    for e in range(4):
        out_core(e).wait_send()


def window(latent, noise, gen_step, critic_step, gen_in, gen_out_t, embed, out, weight):
    smem = pl.BlockSpec(memory_space=pltpu.SMEM)
    return pl.pallas_call(
        window_kernel,
        out_shape=(
            jax.ShapeDtypeStruct((32, 128), F32),
            jax.ShapeDtypeStruct((4, 8, 2, 80, 128), BF16),
        ),
        in_specs=vmem(2) + [smem, smem] + vmem(4) + [pl.BlockSpec(memory_space=pl.ANY)],
        out_specs=tuple(vmem(2)),
        scratch_shapes=[
            pltpu.VMEM((64, D), F32),
            pltpu.VMEM((32, 128), BF16),
            pltpu.VMEM((8, 4, 32, 128), BF16),
            pltpu.VMEM((4, CHUNK, 3 * HD), BF16),
            pltpu.VMEM((ROWS, 3 * HD), F32),
            pltpu.VMEM((ROWS, 128), F32),
            pltpu.VMEM((ROWS, 2 * HD), BF16),
            pltpu.VMEM((2 * ROWS, 2 * HD), BF16),
            pltpu.VMEM((2 * ROWS, 2 * HD), BF16),
            pltpu.VMEM((2 * HD, 128), BF16),
            pltpu.VMEM((2, 64, 128), BF16),
            pltpu.VMEM((8, 128, 128), BF16),
            pltpu.VMEM((4, 8, 32, 128), BF16),
            pltpu.VMEM((4, 8, 32, 128), BF16),
            pltpu.VMEM((7, 128, 128), BF16),
            pltpu.VMEM((4, 32, 128), F32),
            pltpu.VMEM((8, 32, 128), F32),
            pltpu.VMEM((160, 1024), F32),
            pltpu.VMEM((160, 1024), F32),
            pltpu.VMEM((160, 1024), BF16),
            pltpu.VMEM((2, 88, 128), F32),
            pltpu.VMEM((8, 88, 128), F32),
            pltpu.VMEM((4, 8, 2, 80, 128), BF16),
            pltpu.VMEM((32, 64), F32),
            pltpu.VMEM((160, 128), BF16),
            pltpu.VMEM((160, 128), BF16),
            pltpu.SemaphoreType.DMA((N_SEM,)),
            pltpu.SemaphoreType.DMA((N_SEM,)),
            pltpu.SemaphoreType.DMA((1,)),
        ],
        compiler_params=pltpu.CompilerParams(
            collective_id=0, has_side_effects=True, vmem_limit_bytes=56 << 20
        ),
    )(latent, noise, gen_step, critic_step, gen_in, gen_out_t, embed, out, weight)


TURN = 1280


def unpack_kernel(dmd_ref, grads_ref, dmd_out, in_out, out_out):
    dmd_out[:32] = dmd_ref[:, :64]
    dmd_out[32:] = dmd_ref[:, 64:]
    row = lax.broadcasted_iota(jnp.int32, (128, 128), 0)
    col = lax.broadcasted_iota(jnp.int32, (128, 128), 1)
    same = jnp.where(row == col, 1.0, 0.0).astype(BF16)
    turned = dot_nt(same, grads_ref[...])
    in_out[...] = turned[:64]
    out_out[...] = turned[64:]


def unpack(dmd, grads):
    turned = pl.BlockSpec((64, TURN), lambda t: (0, t))
    return pl.pallas_call(
        unpack_kernel,
        grid=(D // TURN,),
        out_shape=(
            jax.ShapeDtypeStruct((64, 64), F32),
            jax.ShapeDtypeStruct((64, D), F32),
            jax.ShapeDtypeStruct((64, D), F32),
        ),
        in_specs=[pl.BlockSpec((32, 128), lambda t: (0, 0)), pl.BlockSpec((TURN, 128), lambda t: (t, 0))],
        out_specs=(pl.BlockSpec((64, 64), lambda t: (0, 0)), turned, turned),
        compiler_params=pltpu.CompilerParams(vmem_limit_bytes=60 << 20),
    )(dmd, grads)


def per_device(
    gen_input, noise, gen_step, critic_step, gen_in, gen_out, critic_embed, critic_qkv, critic_out
):
    weight = critic_qkv.reshape(2, CHUNK, 3 * HD)
    dmd, grads = window(
        gen_input[0], noise[0], gen_step, critic_step, gen_in, gen_out.T, critic_embed[0],
        critic_out[0, 0], weight,
    )
    dmd, grad_in, grad_out = unpack(dmd, grads.reshape(D, 128))
    return (dmd[None], grad_in, grad_out.T)


def solution(mesh):
    return jax.shard_map(
        per_device,
        mesh=mesh,
        in_specs=(
            P("dp", "seq", None),
            P("dp", "seq", None),
            P("dp"),
            P("dp"),
            P(),
            P(),
            P("grp", None, None),
            P("grp", "seq", None, None),
            P("grp", "seq", None, None),
        ),
        out_specs=(P("dp", "seq", None), P(), P()),
        check_vma=False,
    )
```

```python
import jax
import jax.numpy as jnp
from jax import lax
from jax.experimental import pallas as pl
from jax.experimental.pallas import tpu as pltpu
from jax.sharding import PartitionSpec as P

F32 = jnp.float32
BF16 = jnp.bfloat16
NT = 1000
D = 5120
HALF = 2560
LAT = 64
HD = 128
ROWS = 2048
TILE = 256
PART = 320
CHUNK = 1280
SHIFT_VALUE = 5.0
EPS_NORM = 1e-06
EPS_SPREAD = 1e-06
COUNT = 4096 * 64
GA = 0.7978845608028654
GB = GA * 0.044715
SCORE_SCALE = 1.4426950408889634 * HD**-0.5
MESH = pl.DeviceIdType.MESH
CONTRACT_LAST = (((1,), (1,)), ((), ()))


def dot(a, b):
    return jnp.dot(a, b, preferred_element_type=F32)


def dot_nt(a, b):
    return lax.dot_general(a, b, CONTRACT_LAST, preferred_element_type=F32)


def place():
    b = lax.axis_index("grp")
    s = lax.axis_index("seq")
    c = lax.axis_index("dp")
    return b, s // 32, (s // 4) % 8, s % 4, c


def seq_of(xh, z, y):
    return xh * 32 + z * 4 + y


def remote(src, dst, send, recv, device):
    return pltpu.make_async_remote_copy(
        src_ref=src, dst_ref=dst, send_sem=send, recv_sem=recv, device_id=device, device_id_type=MESH
    )


def greet(barrier, device):
    pl.semaphore_signal(barrier, inc=1, device_id=device, device_id_type=MESH)


def sigma_rows(step_ref):
    step = jnp.full((8, 128), step_ref[0], jnp.int32).astype(F32)
    frac = (step + 1.0) / NT
    return (SHIFT_VALUE * frac / (1.0 + (SHIFT_VALUE - 1.0) * frac))[0:1, :]


def split2(value):
    high = value.astype(BF16)
    low = (value - high.astype(F32)).astype(BF16)
    return high, low


def pack(value):
    return jnp.concatenate([value[:32], value[32:]], axis=1)


def vmem(n):
    return [pl.BlockSpec(memory_space=pltpu.VMEM)] * n


def features(x):
    return x + x * jnp.tanh(x * (GA + GB * (x * x)))


ORDER = (0, 1, 7, 2, 6, 3, 5, 4)
STEPS = ((0, 0, 1280), (1, 0, 1280), (2, 0, 640), (3, 0, 640), (2, 640, 640), (3, 640, 640))
W_Y, W_C, U_Y, G_X, G_Z, E_Z, E_Y, K_C = 0, 126, 4, 5, 9, 16, 24, 28
A_Z, B_X, L_Z, L_Y, X_X, F_Z, F_Y, F_C, N_SEM = 34, 42, 50, 58, 82, 90, 98, 122, 130


def window_kernel(
    lat_ref, noise_ref, gs_ref, cs_ref, gin_ref, gout_ref, embed_ref, out_ref, weight_ref,
    dmd_out, in_out, out_out,
    pre_s, mine_s, rows_s, w_s, acc, ssq, qq, kk, vv, uu, um, vel_s,
    eb, lb, arrive_a, part_b, arrive_b, n_s, slope_s, hid_s, piece_s, arrive_x, fin,
    q_s, gi_s, go_s, send, recv, local,
):
    b, xh, z, y, c = place()
    j = y % 2
    y_high = y // 2
    is_self = jnp.logical_and(j == c, y_high == c)
    barrier = pltpu.get_barrier_semaphore()
    me = (b, seq_of(xh, z, y), c)
    sibling = (b, seq_of(xh, z, y), 1 - c)
    partner = (b, seq_of(xh, z, y + 1 - 2 * j), c)

    def at_z(d):
        return (b, seq_of(xh, (z + d) % 8, y), c)

    def at_y(d):
        return (b, seq_of(xh, z, (y + d) % 4), c)

    def at_x(k):
        return ((b + k // 4) % 2, seq_of((xh + k // 2 % 2) % 2, z, y), (c + k % 2) % 2)

    def source_g_self(k):
        return jnp.logical_and(is_self, jnp.logical_and(xh == k // 2, j == k % 2))

    def target_g_self(k):
        return jnp.logical_and(is_self, jnp.logical_and(xh == k // 2, y_high == k % 2))

    def source_b_self(k):
        return jnp.logical_and(target_g_self(k % 4), b == k // 4)

    def target_b_self(k):
        return jnp.logical_and(source_g_self(k % 4), b == k // 4)

    for k in range(4):
        @pl.when(jnp.logical_not(source_g_self(k)))
        def _():
            greet(barrier, (b, seq_of(k // 2, z, 2 * c + k % 2), j))

    for k in range(8):
        @pl.when(jnp.logical_not(source_b_self(k)))
        def _():
            greet(barrier, (k // 4, seq_of(k // 2 % 2, z, c + 2 * (k % 2)), y_high))

    for d in range(1, 8):
        greet(barrier, at_z(d))
        greet(barrier, at_x(d))
    for d in range(1, 4):
        greet(barrier, at_y(d))
    own_weight = pltpu.make_async_copy(weight_ref, w_s.at[pl.ds(0, 2)], local.at[0])
    own_weight.start()

    sg = sigma_rows(gs_ref)
    sc = sigma_rows(cs_ref)
    lat = lat_ref[...]
    um[0] = jnp.concatenate([out_ref[...], jnp.zeros((64, 64), BF16)], axis=1)
    squares = jnp.zeros((64, 128), F32)
    width = 512
    for t in range(D // width):
        cols = slice(t * width, (t + 1) * width)
        pre = dot(lat, gin_ref[:, cols])
        pre_s[:, cols] = pre
        sq = pre * pre
        for u in range(width // 128):
            squares = squares + sq[:, u * 128 : (u + 1) * 128]
    scale = lax.rsqrt(jnp.sum(squares, axis=-1, keepdims=True) / D + EPS_NORM)

    def weight_copy(q):
        rows = pl.ds(q * PART, PART)
        return remote(
            weight_ref.at[c, rows], w_s.at[2, rows], send.at[W_Y + q], recv.at[W_Y + q], partner
        )

    def weight_forward(q):
        rows = pl.ds(q * PART, PART)
        return remote(w_s.at[2, rows], w_s.at[3, rows], send.at[W_C + q], recv.at[W_C + q], sibling)

    out_copy = remote(um.at[0], um.at[1], send.at[U_Y], recv.at[U_Y], partner)

    out = jnp.zeros((64, LAT), F32)
    for t in range(D // width):
        cols = slice(t * width, (t + 1) * width)
        n = pre_s[:, cols] * scale
        th = jnp.tanh(n * (GA + GB * (n * n)))
        out = out + dot_nt((0.5 * n * (1.0 + th)).astype(BF16), gout_ref[:, cols])
    lat_f = lat.astype(F32)
    clean = lat_f - sg[:, :64] * out
    noisy = ((1.0 - sc[:, :64]) * clean + sc[:, :64] * noise_ref[...].astype(F32)).astype(BF16)
    mine = pack(noisy)
    mine_s[...] = mine
    slot = xh * 2 + j

    @pl.when(is_self)
    def _():
        rows_s[0, slot] = mine

    pl.semaphore_wait(barrier, 29 - 2 * is_self.astype(jnp.int32))

    def first(k):
        device = (b, seq_of(k // 2, z, c + 2 * (k % 2)), y_high)
        return remote(mine_s, rows_s.at[0, slot], send.at[G_X + k], recv.at[G_X + slot], device)

    for k in range(4):
        @pl.when(jnp.logical_not(target_g_self(k)))
        def _():
            first(k).start()

    clean = pack(clean)
    high, low = split2(lat_f * scale)
    early = jnp.concatenate([high, low], axis=1)
    eb[0, 0] = jnp.where(b == 0, early[:32], early[32:])

    for k in range(4):
        @pl.when(jnp.logical_not(source_g_self(k)))
        def _():
            remote(mine_s, rows_s.at[0, k], send.at[G_X + k], recv.at[G_X + k], me).wait_recv()

    def second(p):
        d = ORDER[p]
        return remote(
            rows_s.at[0], rows_s.at[p], send.at[G_Z + p - 1], recv.at[G_Z + p - 1], at_z(d)
        )

    for p in range(1, 8):
        second(p).start()

    def along_z(buf, base, d):
        return remote(buf.at[0, 0], buf.at[0, d], send.at[base + d], recv.at[base + d], at_z(d))

    def early_y(d):
        return remote(eb.at[0], eb.at[d], send.at[E_Y + d], recv.at[E_Y + d], at_y(d))

    def late_y(e, d):
        n = L_Y + (e - 1) * 8 + d
        return remote(lb.at[0, d], lb.at[e, d], send.at[n], recv.at[n], at_y(e))

    out_copy.start()
    for d in range(1, 8):
        along_z(eb, E_Z, d).start()
    for q in range(4):
        weight_copy(q).start()

    vv[:, HD:] = jnp.ones((2 * ROWS, HD), BF16)
    own_weight.wait()

    def key_copy(side, part):
        rows = pl.ds(side * 1024, 1024)
        there = pl.ds(ROWS + side * 1024, 1024)
        n = K_C + side * 3 + part
        if part == 2:
            return remote(vv.at[rows, pl.ds(0, HD)], vv.at[there, pl.ds(0, HD)], send.at[n], recv.at[n], sibling)
        return remote(
            kk.at[rows, pl.ds(0, HD)], kk.at[there, pl.ds(part * HD, HD)], send.at[n], recv.at[n], sibling
        )

    starts = (j * HALF, j * HALF + CHUNK, (1 - j) * HALF + c * CHUNK, (1 - j) * HALF + (1 - c) * CHUNK)
    last = len(STEPS) - 1
    for f, (block, low_row, size) in enumerate(STEPS):
        embed = embed_ref[:, pl.ds(pl.multiple_of(starts[block] + low_row, 128), size)]
        if f == 1:
            weight_copy(0).wait_recv()
            weight_forward(0).start()
            for d in range(1, 8):
                along_z(eb, E_Z, d).wait_recv()
            for d in range(1, 4):
                early_y(d).start()
        if f == 2:
            qv = jnp.zeros((64, LAT), F32)
            for t in range(D // width):
                cols = slice(t * width, (t + 1) * width)
                n = pre_s[:, cols] * scale
                n2 = n * n
                th = jnp.tanh(n * (GA + GB * n2))
                slope = 0.5 * (1.0 + th) + 0.5 * n * (1.0 - th * th) * (GA + 3.0 * GB * n2)
                qv = qv + dot_nt((slope * n).astype(BF16), gout_ref[:, cols])
            q_s[...] = jnp.where(b == 0, qv[:32], qv[32:])

            start = (y * 8 + z) * 160
            window = pl.ds(pl.multiple_of(start // 128 * 128, 128), 256)
            row = lax.broadcasted_iota(jnp.int32, (160, 256), 0)
            col = lax.broadcasted_iota(jnp.int32, (160, 256), 1)
            choose = jnp.where(col == row + start % 128, 1.0, 0.0).astype(BF16)
            cut = gin_ref[:, window]
            gi_s[...] = dot_nt(choose, jnp.concatenate([cut, cut], axis=0)).astype(BF16)
            cut = gout_ref[:, window]
            go_s[...] = dot_nt(choose, jnp.concatenate([cut, jnp.zeros_like(cut)], axis=0)).astype(BF16)

            weight_copy(1).wait_recv()
            weight_forward(1).start()
        if f == 3:
            weight_copy(2).wait_recv()
            weight_forward(2).start()
            weight_forward(0).wait_recv()
            weight_forward(1).wait_recv()
        if f == 4:
            weight_copy(3).wait_recv()
            weight_forward(3).start()
        if f == 5:
            weight_forward(2).wait_recv()
            weight_forward(3).wait_recv()

        def activate(t):
            side, part = t // 4, t % 4
            if f == 0 and side == 0:
                for p in (2 * part, 2 * part + 1):
                    if p > 0:
                        second(p).wait_recv()
            tile = rows_s[2 * part : 2 * part + 2].reshape(TILE, 128)
            x = dot(tile[:, side * 64 : (side + 1) * 64], embed)
            e = features(x)
            squares = e * e
            total = squares[:, :128]
            for u in range(1, size // 128):
                total = total + squares[:, u * 128 : (u + 1) * 128]
            rows = slice(t * TILE, (t + 1) * TILE)
            ssq[rows, :] = total if f == 0 else ssq[rows, :] + total
            return e.astype(BF16)

        def accumulate(t, e):
            rows = slice(t * TILE, (t + 1) * TILE)
            got = dot(e, w_s[block, low_row : low_row + size])
            if f > 0:
                got = got + acc[rows, :]
            if f < last:
                acc[rows, :] = got
                return
            mean = jnp.sum(ssq[rows, :], axis=-1, keepdims=True) / D
            got = (got * lax.rsqrt(mean + 4.0 * EPS_NORM)).astype(BF16)
            qq[rows, :] = jnp.concatenate(split2(got[:, :HD].astype(F32) * SCORE_SCALE), axis=1)
            kk[rows, :] = jnp.concatenate([got[:, HD : 2 * HD]] * 2, axis=1)
            vv[rows, :HD] = got[:, 2 * HD :]
            if t % 4 == 3:
                for part in range(3):
                    key_copy(t // 4, part).start()

        before = activate(0)
        for t in range(1, 8):
            now = activate(t)
            accumulate(t - 1, before)
            before = now
        accumulate(7, before)

    out_copy.wait_recv()
    own = um[0][:, :64]
    other = um[1][:, :64]
    full = jnp.concatenate([jnp.where(j == 0, own, other), jnp.where(j == 0, other, own)], axis=0)
    none = jnp.zeros((HD, LAT), BF16)
    uu[:HD, :] = jnp.concatenate([full, none], axis=1)
    uu[HD:, :] = jnp.concatenate([none, full], axis=1)
    for side in range(2):
        for part in range(3):
            key_copy(side, part).wait_recv()

    def vel_copy(p):
        e = (8 - ORDER[p]) % 8
        return remote(vel_s.at[p], arrive_a.at[e - 1], send.at[A_Z + e], recv.at[A_Z + e], at_z(e))

    def scores(p):
        query = jnp.concatenate(
            [qq[p * 128 : (p + 1) * 128, :], qq[1024 + p * 128 : 1024 + (p + 1) * 128, :]], axis=0
        )
        return dot_nt(query, kk[...])

    def mix(s):
        top = jnp.max(s, axis=-1, keepdims=True)
        got = dot(jnp.exp2(s - top).astype(BF16), vv[...])
        attended = (got[:, :HD] / got[:, HD:]).astype(BF16)
        return jnp.concatenate([attended[:128], attended[128:]], axis=1)

    def velocity(p, both):
        vel_s[p] = dot(both, uu[...]).astype(BF16)
        if p > 0:
            vel_copy(p).start()

    s_next = scores(7)
    both = None
    for p in range(7, -1, -1):
        s_now = s_next
        if p > 0:
            s_next = scores(p - 1)
        if both is not None:
            velocity(p + 1, both)
        both = mix(s_now)
    velocity(0, both)

    total = vel_s[0].astype(F32)
    for p in range(7, 0, -1):
        vel_copy(p).wait_recv()
        total = total + arrive_a[(8 - ORDER[p]) % 8 - 1].astype(F32)
    for k in range(4):
        part_b[k] = total[k * 32 : (k + 1) * 32]
    slot_b = b * 4 + xh * 2 + y_high

    def part_copy(k):
        device = (k // 4, seq_of(k // 2 % 2, z, 2 * c + k % 2), j)
        return remote(part_b.at[k % 4], arrive_b.at[slot_b], send.at[B_X + k], recv.at[B_X + slot_b], device)

    for k in range(8):
        @pl.when(jnp.logical_not(target_b_self(k)))
        def _():
            part_copy(k).start()

        @pl.when(target_b_self(k))
        def _():
            arrive_b[slot_b] = part_b[k % 4]

    for d in range(1, 4):
        early_y(d).wait_recv()
    early = eb[...].reshape(1024, 128)
    n = dot_nt(gi_s[...], early)
    n2 = n * n
    th = jnp.tanh(n * (GA + GB * n2))
    n_s[...] = n
    hid_s[...] = (0.5 * n * (1.0 + th)).astype(BF16)
    slope_s[...] = 0.5 * (1.0 + th) + 0.5 * n * (1.0 - th * th) * (GA + 3.0 * GB * n2)

    for k in range(8):
        @pl.when(jnp.logical_not(source_b_self(k)))
        def _():
            remote(
                part_b.at[k % 4], arrive_b.at[k], send.at[B_X + k], recv.at[B_X + k], me
            ).wait_recv()

    teacher = arrive_b[0] + arrive_b[1] + arrive_b[2] + arrive_b[3]
    fake = arrive_b[4] + arrive_b[5] + arrive_b[6] + arrive_b[7]
    gap = fake - teacher
    away = jnp.abs(clean - (mine_s[...].astype(F32) - sc * teacher))
    my_gap = jnp.where(b == 0, gap[:, :64], gap[:, 64:])
    my_away = jnp.where(b == 0, away[:, :64], away[:, 64:])
    away_row = jnp.sum(my_away, axis=-1, keepdims=True)
    rbar = jnp.sum(my_gap * q_s[...], axis=-1, keepdims=True) / D
    r_high, r_low = split2(rbar)
    a_high, a_low = split2(away_row)
    a_rest = (away_row - a_high.astype(F32) - a_low.astype(F32)).astype(BF16)
    lane = lax.broadcasted_iota(jnp.int32, (32, 64), 1)
    extra = jnp.zeros((32, 64), F32)
    for at, value in enumerate((r_high, r_low, a_high, a_low, a_rest)):
        extra = jnp.where(lane == at, value.astype(F32), extra)
    lb[0, 0] = jnp.concatenate([my_gap, extra], axis=1).astype(BF16)

    for d in range(1, 8):
        along_z(lb, L_Z, d).start()
    for e in range(1, 4):
        late_y(e, 0).start()
    for d in ORDER[1:]:
        along_z(lb, L_Z, d).wait_recv()
        for e in range(1, 4):
            late_y(e, d).start()
    for d in range(8):
        for e in range(1, 4):
            late_y(e, d).wait_recv()
    late = lb[...].reshape(1024, 128)
    lane = lax.broadcasted_iota(jnp.int32, (16, 128), 1)
    pick = jnp.where(jnp.logical_or(lane == 64, lane == 65), 1.0, 0.0).astype(BF16)
    rbar_all = dot_nt(pick, late)[0:1, :]
    away_all = dot(jnp.ones((16, 1024), BF16), late)[0:1, :]
    lane1 = lax.broadcasted_iota(jnp.int32, (1, 128), 1)
    away_sum = jnp.sum(
        jnp.where(jnp.logical_and(lane1 >= 66, lane1 <= 68), away_all, 0.0), axis=-1, keepdims=True
    )
    dpre = (slope_s[...] * dot_nt(go_s[...], late) - n_s[...] * rbar_all).astype(BF16)
    grad_in = dot(dpre, early)
    grad_out = dot(hid_s[...], late)
    piece = jnp.concatenate([grad_in[:, :64] + grad_in[:, 64:], grad_out[:, :64]], axis=1)
    row8 = lax.broadcasted_iota(jnp.int32, (8, 128), 0)
    extra8 = jnp.where(row8 == 0, away_sum, sg * sc)
    for p in range(2):
        piece_s[p, :80] = piece[p * 80 : (p + 1) * 80]
        piece_s[p, 80:] = extra8

    def piece_copy(k):
        return remote(
            piece_s.at[(c + k % 2) % 2], arrive_x.at[k], send.at[X_X + k], recv.at[X_X + k], at_x(k)
        )

    for k in range(1, 8):
        piece_copy(k).start()
    arrive_x[0] = piece_s[c]
    for k in range(1, 8):
        piece_copy(k).wait_recv()
    same = arrive_x[0] + arrive_x[2] + arrive_x[4] + arrive_x[6]
    cross = arrive_x[1] + arrive_x[3] + arrive_x[5] + arrive_x[7]
    spread = same[80:81] / COUNT + EPS_SPREAD
    spread_cross = cross[80:81] / COUNT + EPS_SPREAD
    result = (0.25 * same[81:82] / spread) * same[:80] + (0.25 * cross[81:82] / spread_cross) * cross[:80]
    fin[y, z, c] = result.astype(BF16)

    def out_z(d):
        at = fin.at[y, z, c]
        return remote(at, at, send.at[F_Z + d], recv.at[F_Z + d], at_z(d))

    def out_z_here(d):
        at = fin.at[y, (z + 8 - d) % 8, c]
        return remote(at, at, send.at[F_Z + d], recv.at[F_Z + d], at_z(d))

    def out_y(e, d):
        n = F_Y + (e - 1) * 8 + d
        at = fin.at[y, (z + 8 - d) % 8, c]
        return remote(at, at, send.at[n], recv.at[n], at_y(e))

    def out_y_here(e, d):
        n = F_Y + (e - 1) * 8 + d
        at = fin.at[(y + 4 - e) % 4, (z + 8 - d) % 8, c]
        return remote(at, at, send.at[n], recv.at[n], at_y(e))

    def out_core(e):
        at = fin.at[(y + 4 - e) % 4, :, c]
        return remote(at, at, send.at[F_C + e], recv.at[F_C + e], sibling)

    def out_core_here(e):
        at = fin.at[(y + 4 - e) % 4, :, 1 - c]
        return remote(at, at, send.at[F_C + e], recv.at[F_C + e], sibling)

    for d in range(1, 8):
        out_z(d).start()
    for e in range(1, 4):
        out_y(e, 0).start()
    dmd = -sc * gap / spread
    dmd_out[:32] = dmd[:, :64]
    dmd_out[32:] = dmd[:, 64:]
    row = lax.broadcasted_iota(jnp.int32, (128, 128), 0)
    col = lax.broadcasted_iota(jnp.int32, (128, 128), 1)
    same_index = jnp.where(row == col, 1.0, 0.0).astype(BF16)

    def turn(e):
        out_core_here(e).wait_recv()
        at_row = (y + 4 - e) % 4
        turned = dot_nt(same_index, fin[at_row].reshape(1280, 128))
        cols = pl.ds(pl.multiple_of(at_row * 1280, 128), 1280)
        in_out[:, cols] = turned[:64]
        out_out[:, cols] = turned[64:]

    for d in ORDER[1:]:
        out_z_here(d).wait_recv()
        for e in range(1, 4):
            out_y(e, d).start()
    out_core(0).start()
    for e in (1, 3, 2):
        for d in range(8):
            out_y_here(e, d).wait_recv()
        out_core(e).start()
        turn({1: 0, 3: 1, 2: 3}[e])
    turn(2)

    for k in range(4):
        @pl.when(jnp.logical_not(target_g_self(k)))
        def _():
            first(k).wait_send()
    for k in range(8):
        @pl.when(jnp.logical_not(target_b_self(k)))
        def _():
            part_copy(k).wait_send()
    for q in range(4):
        weight_copy(q).wait_send()
        weight_forward(q).wait_send()
    for side in range(2):
        for part in range(3):
            key_copy(side, part).wait_send()
    out_copy.wait_send()
    for d in range(1, 8):
        second(d).wait_send()
        along_z(eb, E_Z, d).wait_send()
        vel_copy(d).wait_send()
        along_z(lb, L_Z, d).wait_send()
        piece_copy(d).wait_send()
        out_z(d).wait_send()
    for e in range(1, 4):
        early_y(e).wait_send()
        for d in range(8):
            late_y(e, d).wait_send()
            out_y(e, d).wait_send()
    for e in range(4):
        out_core(e).wait_send()


def window(latent, noise, gen_step, critic_step, gen_in, gen_out_t, embed, out, weight):
    smem = pl.BlockSpec(memory_space=pltpu.SMEM)
    return pl.pallas_call(
        window_kernel,
        out_shape=(
            jax.ShapeDtypeStruct((64, 64), F32),
            jax.ShapeDtypeStruct((64, D), F32),
            jax.ShapeDtypeStruct((64, D), F32),
        ),
        in_specs=vmem(2) + [smem, smem] + vmem(4) + [pl.BlockSpec(memory_space=pl.ANY)],
        out_specs=tuple(vmem(3)),
        scratch_shapes=[
            pltpu.VMEM((64, D), F32),
            pltpu.VMEM((32, 128), BF16),
            pltpu.VMEM((8, 4, 32, 128), BF16),
            pltpu.VMEM((4, CHUNK, 3 * HD), BF16),
            pltpu.VMEM((ROWS, 3 * HD), F32),
            pltpu.VMEM((ROWS, 128), F32),
            pltpu.VMEM((ROWS, 2 * HD), BF16),
            pltpu.VMEM((2 * ROWS, 2 * HD), BF16),
            pltpu.VMEM((2 * ROWS, 2 * HD), BF16),
            pltpu.VMEM((2 * HD, 128), BF16),
            pltpu.VMEM((2, 64, 128), BF16),
            pltpu.VMEM((8, 128, 128), BF16),
            pltpu.VMEM((4, 8, 32, 128), BF16),
            pltpu.VMEM((4, 8, 32, 128), BF16),
            pltpu.VMEM((7, 128, 128), BF16),
            pltpu.VMEM((4, 32, 128), F32),
            pltpu.VMEM((8, 32, 128), F32),
            pltpu.VMEM((160, 1024), F32),
            pltpu.VMEM((160, 1024), F32),
            pltpu.VMEM((160, 1024), BF16),
            pltpu.VMEM((2, 88, 128), F32),
            pltpu.VMEM((8, 88, 128), F32),
            pltpu.VMEM((4, 8, 2, 80, 128), BF16),
            pltpu.VMEM((32, 64), F32),
            pltpu.VMEM((160, 128), BF16),
            pltpu.VMEM((160, 128), BF16),
            pltpu.SemaphoreType.DMA((N_SEM,)),
            pltpu.SemaphoreType.DMA((N_SEM,)),
            pltpu.SemaphoreType.DMA((1,)),
        ],
        compiler_params=pltpu.CompilerParams(
            collective_id=0, has_side_effects=True, vmem_limit_bytes=56 << 20
        ),
    )(latent, noise, gen_step, critic_step, gen_in, gen_out_t, embed, out, weight)


def per_device(
    gen_input, noise, gen_step, critic_step, gen_in, gen_out, critic_embed, critic_qkv, critic_out
):
    weight = critic_qkv.reshape(2, CHUNK, 3 * HD)
    dmd, grad_in, grad_out = window(
        gen_input[0], noise[0], gen_step, critic_step, gen_in, gen_out.T, critic_embed[0],
        critic_out[0, 0], weight,
    )
    return (dmd[None], grad_in, grad_out.T)


def solution(mesh):
    return jax.shard_map(
        per_device,
        mesh=mesh,
        in_specs=(
            P("dp", "seq", None),
            P("dp", "seq", None),
            P("dp"),
            P("dp"),
            P(),
            P(),
            P("grp", None, None),
            P("grp", "seq", None, None),
            P("grp", "seq", None, None),
        ),
        out_specs=(P("dp", "seq", None), P(), P()),
        check_vma=False,
    )
```

```python
import jax
import jax.numpy as jnp
from jax import lax
from jax.experimental import pallas as pl
from jax.experimental.pallas import tpu as pltpu
from jax.sharding import PartitionSpec as P

F32 = jnp.float32
BF16 = jnp.bfloat16
NT = 1000
D = 5120
HALF = 2560
LAT = 64
HD = 128
ROWS = 2048
TILE = 256
PART = 320
CHUNK = 1280
SHIFT_VALUE = 5.0
EPS_NORM = 1e-06
EPS_SPREAD = 1e-06
COUNT = 4096 * 64
GA = 0.7978845608028654
GB = GA * 0.044715
SCORE_SCALE = 1.4426950408889634 * HD**-0.5
MESH = pl.DeviceIdType.MESH
CONTRACT_LAST = (((1,), (1,)), ((), ()))


def dot(a, b):
    return jnp.dot(a, b, preferred_element_type=F32)


def dot_nt(a, b):
    return lax.dot_general(a, b, CONTRACT_LAST, preferred_element_type=F32)


def place():
    b = lax.axis_index("grp")
    s = lax.axis_index("seq")
    c = lax.axis_index("dp")
    return b, s // 32, (s // 4) % 8, s % 4, c


def seq_of(xh, z, y):
    return xh * 32 + z * 4 + y


def remote(src, dst, send, recv, device):
    return pltpu.make_async_remote_copy(
        src_ref=src, dst_ref=dst, send_sem=send, recv_sem=recv, device_id=device, device_id_type=MESH
    )


def greet(barrier, device):
    pl.semaphore_signal(barrier, inc=1, device_id=device, device_id_type=MESH)


def sigma_rows(step_ref):
    step = jnp.full((8, 128), step_ref[0], jnp.int32).astype(F32)
    frac = (step + 1.0) / NT
    return (SHIFT_VALUE * frac / (1.0 + (SHIFT_VALUE - 1.0) * frac))[0:1, :]


def split2(value):
    high = value.astype(BF16)
    low = (value - high.astype(F32)).astype(BF16)
    return high, low


def pack(value):
    return jnp.concatenate([value[:32], value[32:]], axis=1)


def vmem(n):
    return [pl.BlockSpec(memory_space=pltpu.VMEM)] * n


def features(x):
    return x + x * jnp.tanh(x * (GA + GB * (x * x)))


ORDER = (0, 1, 7, 2, 6, 3, 5, 4)
STEPS = ((0, 0, 1280), (1, 0, 1280), (2, 0, 640), (3, 0, 640), (2, 640, 640), (3, 640, 640))
W_Y, W_C, U_Y, G_X, G_Z, E_Z, E_Y, K_C = 0, 126, 4, 5, 9, 16, 24, 28
A_Z, B_X, L_Z, L_Y, X_X, F_Z, F_Y, F_C, N_SEM = 34, 42, 50, 58, 82, 90, 98, 122, 130


def window_kernel(
    lat_ref, noise_ref, gs_ref, cs_ref, gin_ref, gout_ref, embed_ref, out_ref, weight_ref,
    dmd_out, in_out, out_out,
    pre_s, mine_s, rows_s, w_s, acc, ssq, qq, kk, vv, uu, um, vel_s,
    eb, lb, arrive_a, part_b, arrive_b, n_s, slope_s, hid_s, piece_s, arrive_x, fin,
    q_s, gi_s, go_s, send, recv, local,
):
    b, xh, z, y, c = place()
    j = y % 2
    y_high = y // 2
    is_self = jnp.logical_and(j == c, y_high == c)
    barrier = pltpu.get_barrier_semaphore()
    me = (b, seq_of(xh, z, y), c)
    sibling = (b, seq_of(xh, z, y), 1 - c)
    partner = (b, seq_of(xh, z, y + 1 - 2 * j), c)

    def at_z(d):
        return (b, seq_of(xh, (z + d) % 8, y), c)

    def at_y(d):
        return (b, seq_of(xh, z, (y + d) % 4), c)

    def at_x(k):
        return ((b + k // 4) % 2, seq_of((xh + k // 2 % 2) % 2, z, y), (c + k % 2) % 2)

    def source_g_self(k):
        return jnp.logical_and(is_self, jnp.logical_and(xh == k // 2, j == k % 2))

    def target_g_self(k):
        return jnp.logical_and(is_self, jnp.logical_and(xh == k // 2, y_high == k % 2))

    def source_b_self(k):
        return jnp.logical_and(target_g_self(k % 4), b == k // 4)

    def target_b_self(k):
        return jnp.logical_and(source_g_self(k % 4), b == k // 4)

    for k in range(4):
        @pl.when(jnp.logical_not(source_g_self(k)))
        def _():
            greet(barrier, (b, seq_of(k // 2, z, 2 * c + k % 2), j))

    for k in range(8):
        @pl.when(jnp.logical_not(source_b_self(k)))
        def _():
            greet(barrier, (k // 4, seq_of(k // 2 % 2, z, c + 2 * (k % 2)), y_high))

    for d in range(1, 8):
        greet(barrier, at_z(d))
        greet(barrier, at_x(d))
    for d in range(1, 4):
        greet(barrier, at_y(d))
    own_weight = pltpu.make_async_copy(weight_ref, w_s.at[pl.ds(0, 2)], local.at[0])
    own_weight.start()

    sg = sigma_rows(gs_ref)
    sc = sigma_rows(cs_ref)
    lat = lat_ref[...]
    um[0] = jnp.concatenate([out_ref[...], jnp.zeros((64, 64), BF16)], axis=1)
    squares = jnp.zeros((64, 128), F32)
    width = 512
    for t in range(D // width):
        cols = slice(t * width, (t + 1) * width)
        pre = dot(lat, gin_ref[:, cols])
        pre_s[:, cols] = pre
        sq = pre * pre
        for u in range(width // 128):
            squares = squares + sq[:, u * 128 : (u + 1) * 128]
    scale = lax.rsqrt(jnp.sum(squares, axis=-1, keepdims=True) / D + EPS_NORM)

    def weight_copy(q):
        rows = pl.ds(q * PART, PART)
        return remote(
            weight_ref.at[c, rows], w_s.at[2, rows], send.at[W_Y + q], recv.at[W_Y + q], partner
        )

    def weight_forward(q):
        rows = pl.ds(q * PART, PART)
        return remote(w_s.at[2, rows], w_s.at[3, rows], send.at[W_C + q], recv.at[W_C + q], sibling)

    out_copy = remote(um.at[0], um.at[1], send.at[U_Y], recv.at[U_Y], partner)

    out = jnp.zeros((64, LAT), F32)
    for t in range(D // width):
        cols = slice(t * width, (t + 1) * width)
        n = pre_s[:, cols] * scale
        th = jnp.tanh(n * (GA + GB * (n * n)))
        out = out + dot_nt((0.5 * n * (1.0 + th)).astype(BF16), gout_ref[:, cols])
    lat_f = lat.astype(F32)
    clean = lat_f - sg[:, :64] * out
    noisy = ((1.0 - sc[:, :64]) * clean + sc[:, :64] * noise_ref[...].astype(F32)).astype(BF16)
    mine = pack(noisy)
    mine_s[...] = mine
    slot = xh * 2 + j

    @pl.when(is_self)
    def _():
        rows_s[0, slot] = mine

    pl.semaphore_wait(barrier, 29 - 2 * is_self.astype(jnp.int32))

    def first(k):
        device = (b, seq_of(k // 2, z, c + 2 * (k % 2)), y_high)
        return remote(mine_s, rows_s.at[0, slot], send.at[G_X + k], recv.at[G_X + slot], device)

    for k in range(4):
        @pl.when(jnp.logical_not(target_g_self(k)))
        def _():
            first(k).start()
    weight_copy(0).start()

    clean = pack(clean)
    high, low = split2(lat_f * scale)
    early = jnp.concatenate([high, low], axis=1)
    eb[0, 0] = jnp.where(b == 0, early[:32], early[32:])

    for k in range(4):
        @pl.when(jnp.logical_not(source_g_self(k)))
        def _():
            remote(mine_s, rows_s.at[0, k], send.at[G_X + k], recv.at[G_X + k], me).wait_recv()

    def second(p):
        d = ORDER[p]
        return remote(
            rows_s.at[0], rows_s.at[p], send.at[G_Z + p - 1], recv.at[G_Z + p - 1], at_z(d)
        )

    for p in range(1, 8):
        second(p).start()

    def along_z(buf, base, d):
        return remote(buf.at[0, 0], buf.at[0, d], send.at[base + d], recv.at[base + d], at_z(d))

    def early_y(d):
        return remote(eb.at[0], eb.at[d], send.at[E_Y + d], recv.at[E_Y + d], at_y(d))

    def late_y(e, d):
        n = L_Y + (e - 1) * 8 + d
        return remote(lb.at[0, d], lb.at[e, d], send.at[n], recv.at[n], at_y(e))

    out_copy.start()
    for d in range(1, 8):
        along_z(eb, E_Z, d).start()
    for q in range(1, 4):
        weight_copy(q).start()

    vv[:, HD:] = jnp.ones((2 * ROWS, HD), BF16)
    own_weight.wait()

    def key_copy(side, part):
        rows = pl.ds(side * 1024, 1024)
        there = pl.ds(ROWS + side * 1024, 1024)
        n = K_C + side * 3 + part
        if part == 2:
            return remote(vv.at[rows, pl.ds(0, HD)], vv.at[there, pl.ds(0, HD)], send.at[n], recv.at[n], sibling)
        return remote(
            kk.at[rows, pl.ds(0, HD)], kk.at[there, pl.ds(part * HD, HD)], send.at[n], recv.at[n], sibling
        )

    starts = (j * HALF, j * HALF + CHUNK, (1 - j) * HALF + c * CHUNK, (1 - j) * HALF + (1 - c) * CHUNK)
    last = len(STEPS) - 1
    for f, (block, low_row, size) in enumerate(STEPS):
        embed = embed_ref[:, pl.ds(pl.multiple_of(starts[block] + low_row, 128), size)]
        if f == 1:
            weight_copy(0).wait_recv()
            weight_forward(0).start()
            for d in range(1, 8):
                along_z(eb, E_Z, d).wait_recv()
            for d in range(1, 4):
                early_y(d).start()
        if f == 2:
            qv = jnp.zeros((64, LAT), F32)
            for t in range(D // width):
                cols = slice(t * width, (t + 1) * width)
                n = pre_s[:, cols] * scale
                n2 = n * n
                th = jnp.tanh(n * (GA + GB * n2))
                slope = 0.5 * (1.0 + th) + 0.5 * n * (1.0 - th * th) * (GA + 3.0 * GB * n2)
                qv = qv + dot_nt((slope * n).astype(BF16), gout_ref[:, cols])
            q_s[...] = jnp.where(b == 0, qv[:32], qv[32:])

            start = (y * 8 + z) * 160
            window = pl.ds(pl.multiple_of(start // 128 * 128, 128), 256)
            row = lax.broadcasted_iota(jnp.int32, (160, 256), 0)
            col = lax.broadcasted_iota(jnp.int32, (160, 256), 1)
            choose = jnp.where(col == row + start % 128, 1.0, 0.0).astype(BF16)
            cut = gin_ref[:, window]
            gi_s[...] = dot_nt(choose, jnp.concatenate([cut, cut], axis=0)).astype(BF16)
            cut = gout_ref[:, window]
            go_s[...] = dot_nt(choose, jnp.concatenate([cut, jnp.zeros_like(cut)], axis=0)).astype(BF16)

            weight_copy(1).wait_recv()
            weight_forward(1).start()
        if f == 3:
            weight_copy(2).wait_recv()
            weight_forward(2).start()
            weight_forward(0).wait_recv()
            weight_forward(1).wait_recv()
        if f == 4:
            weight_copy(3).wait_recv()
            weight_forward(3).start()
        if f == 5:
            weight_forward(2).wait_recv()
            weight_forward(3).wait_recv()

        def activate(t):
            side, part = t // 4, t % 4
            if f == 0 and side == 0:
                for p in (2 * part, 2 * part + 1):
                    if p > 0:
                        second(p).wait_recv()
            tile = rows_s[2 * part : 2 * part + 2].reshape(TILE, 128)
            x = dot(tile[:, side * 64 : (side + 1) * 64], embed)
            e = features(x)
            squares = e * e
            total = squares[:, :128]
            for u in range(1, size // 128):
                total = total + squares[:, u * 128 : (u + 1) * 128]
            rows = slice(t * TILE, (t + 1) * TILE)
            ssq[rows, :] = total if f == 0 else ssq[rows, :] + total
            return e.astype(BF16)

        def accumulate(t, e):
            rows = slice(t * TILE, (t + 1) * TILE)
            got = dot(e, w_s[block, low_row : low_row + size])
            if f > 0:
                got = got + acc[rows, :]
            if f < last:
                acc[rows, :] = got
                return
            mean = jnp.sum(ssq[rows, :], axis=-1, keepdims=True) / D
            got = (got * lax.rsqrt(mean + 4.0 * EPS_NORM)).astype(BF16)
            qq[rows, :] = jnp.concatenate(split2(got[:, :HD].astype(F32) * SCORE_SCALE), axis=1)
            kk[rows, :] = jnp.concatenate([got[:, HD : 2 * HD]] * 2, axis=1)
            vv[rows, :HD] = got[:, 2 * HD :]
            if t % 4 == 3:
                for part in range(3):
                    key_copy(t // 4, part).start()

        before = activate(0)
        for t in range(1, 8):
            now = activate(t)
            accumulate(t - 1, before)
            before = now
        accumulate(7, before)

    out_copy.wait_recv()
    own = um[0][:, :64]
    other = um[1][:, :64]
    full = jnp.concatenate([jnp.where(j == 0, own, other), jnp.where(j == 0, other, own)], axis=0)
    none = jnp.zeros((HD, LAT), BF16)
    uu[:HD, :] = jnp.concatenate([full, none], axis=1)
    uu[HD:, :] = jnp.concatenate([none, full], axis=1)
    for side in range(2):
        for part in range(3):
            key_copy(side, part).wait_recv()

    def vel_copy(p):
        e = (8 - ORDER[p]) % 8
        return remote(vel_s.at[p], arrive_a.at[e - 1], send.at[A_Z + e], recv.at[A_Z + e], at_z(e))

    def scores(p):
        query = jnp.concatenate(
            [qq[p * 128 : (p + 1) * 128, :], qq[1024 + p * 128 : 1024 + (p + 1) * 128, :]], axis=0
        )
        return dot_nt(query, kk[...])

    def mix(s):
        top = jnp.max(s, axis=-1, keepdims=True)
        got = dot(jnp.exp2(s - top).astype(BF16), vv[...])
        attended = (got[:, :HD] / got[:, HD:]).astype(BF16)
        return jnp.concatenate([attended[:128], attended[128:]], axis=1)

    def velocity(p, both):
        vel_s[p] = dot(both, uu[...]).astype(BF16)
        if p > 0:
            vel_copy(p).start()

    s_next = scores(7)
    both = None
    for p in range(7, -1, -1):
        s_now = s_next
        if p > 0:
            s_next = scores(p - 1)
        if both is not None:
            velocity(p + 1, both)
        both = mix(s_now)
    velocity(0, both)

    total = vel_s[0].astype(F32)
    for p in range(7, 0, -1):
        vel_copy(p).wait_recv()
        total = total + arrive_a[(8 - ORDER[p]) % 8 - 1].astype(F32)
    for k in range(4):
        part_b[k] = total[k * 32 : (k + 1) * 32]
    slot_b = b * 4 + xh * 2 + y_high

    def part_copy(k):
        device = (k // 4, seq_of(k // 2 % 2, z, 2 * c + k % 2), j)
        return remote(part_b.at[k % 4], arrive_b.at[slot_b], send.at[B_X + k], recv.at[B_X + slot_b], device)

    for k in range(8):
        @pl.when(jnp.logical_not(target_b_self(k)))
        def _():
            part_copy(k).start()

        @pl.when(target_b_self(k))
        def _():
            arrive_b[slot_b] = part_b[k % 4]

    for d in range(1, 4):
        early_y(d).wait_recv()
    early = eb[...].reshape(1024, 128)
    n = dot_nt(gi_s[...], early)
    n2 = n * n
    th = jnp.tanh(n * (GA + GB * n2))
    n_s[...] = n
    hid_s[...] = (0.5 * n * (1.0 + th)).astype(BF16)
    slope_s[...] = 0.5 * (1.0 + th) + 0.5 * n * (1.0 - th * th) * (GA + 3.0 * GB * n2)

    for k in range(8):
        @pl.when(jnp.logical_not(source_b_self(k)))
        def _():
            remote(
                part_b.at[k % 4], arrive_b.at[k], send.at[B_X + k], recv.at[B_X + k], me
            ).wait_recv()

    teacher = arrive_b[0] + arrive_b[1] + arrive_b[2] + arrive_b[3]
    fake = arrive_b[4] + arrive_b[5] + arrive_b[6] + arrive_b[7]
    gap = fake - teacher
    away = jnp.abs(clean - (mine_s[...].astype(F32) - sc * teacher))
    my_gap = jnp.where(b == 0, gap[:, :64], gap[:, 64:])
    my_away = jnp.where(b == 0, away[:, :64], away[:, 64:])
    away_row = jnp.sum(my_away, axis=-1, keepdims=True)
    rbar = jnp.sum(my_gap * q_s[...], axis=-1, keepdims=True) / D
    r_high, r_low = split2(rbar)
    a_high, a_low = split2(away_row)
    a_rest = (away_row - a_high.astype(F32) - a_low.astype(F32)).astype(BF16)
    lane = lax.broadcasted_iota(jnp.int32, (32, 64), 1)
    extra = jnp.zeros((32, 64), F32)
    for at, value in enumerate((r_high, r_low, a_high, a_low, a_rest)):
        extra = jnp.where(lane == at, value.astype(F32), extra)
    lb[0, 0] = jnp.concatenate([my_gap, extra], axis=1).astype(BF16)

    for d in range(1, 8):
        along_z(lb, L_Z, d).start()
    for e in range(1, 4):
        late_y(e, 0).start()
    for d in ORDER[1:]:
        along_z(lb, L_Z, d).wait_recv()
        for e in range(1, 4):
            late_y(e, d).start()
    for d in range(8):
        for e in range(1, 4):
            late_y(e, d).wait_recv()
    late = lb[...].reshape(1024, 128)
    lane = lax.broadcasted_iota(jnp.int32, (16, 128), 1)
    pick = jnp.where(jnp.logical_or(lane == 64, lane == 65), 1.0, 0.0).astype(BF16)
    rbar_all = dot_nt(pick, late)[0:1, :]
    away_all = dot(jnp.ones((16, 1024), BF16), late)[0:1, :]
    lane1 = lax.broadcasted_iota(jnp.int32, (1, 128), 1)
    away_sum = jnp.sum(
        jnp.where(jnp.logical_and(lane1 >= 66, lane1 <= 68), away_all, 0.0), axis=-1, keepdims=True
    )
    dpre = (slope_s[...] * dot_nt(go_s[...], late) - n_s[...] * rbar_all).astype(BF16)
    grad_in = dot(dpre, early)
    grad_out = dot(hid_s[...], late)
    piece = jnp.concatenate([grad_in[:, :64] + grad_in[:, 64:], grad_out[:, :64]], axis=1)
    row8 = lax.broadcasted_iota(jnp.int32, (8, 128), 0)
    extra8 = jnp.where(row8 == 0, away_sum, sg * sc)
    for p in range(2):
        piece_s[p, :80] = piece[p * 80 : (p + 1) * 80]
        piece_s[p, 80:] = extra8

    def piece_copy(k):
        return remote(
            piece_s.at[(c + k % 2) % 2], arrive_x.at[k], send.at[X_X + k], recv.at[X_X + k], at_x(k)
        )

    for k in range(1, 8):
        piece_copy(k).start()
    arrive_x[0] = piece_s[c]
    for k in range(1, 8):
        piece_copy(k).wait_recv()
    same = arrive_x[0] + arrive_x[2] + arrive_x[4] + arrive_x[6]
    cross = arrive_x[1] + arrive_x[3] + arrive_x[5] + arrive_x[7]
    spread = same[80:81] / COUNT + EPS_SPREAD
    spread_cross = cross[80:81] / COUNT + EPS_SPREAD
    result = (0.25 * same[81:82] / spread) * same[:80] + (0.25 * cross[81:82] / spread_cross) * cross[:80]
    fin[y, z, c] = result.astype(BF16)

    def out_z(d):
        at = fin.at[y, z, c]
        return remote(at, at, send.at[F_Z + d], recv.at[F_Z + d], at_z(d))

    def out_z_here(d):
        at = fin.at[y, (z + 8 - d) % 8, c]
        return remote(at, at, send.at[F_Z + d], recv.at[F_Z + d], at_z(d))

    def out_y(e, d):
        n = F_Y + (e - 1) * 8 + d
        at = fin.at[y, (z + 8 - d) % 8, c]
        return remote(at, at, send.at[n], recv.at[n], at_y(e))

    def out_y_here(e, d):
        n = F_Y + (e - 1) * 8 + d
        at = fin.at[(y + 4 - e) % 4, (z + 8 - d) % 8, c]
        return remote(at, at, send.at[n], recv.at[n], at_y(e))

    def out_core(e):
        at = fin.at[(y + 4 - e) % 4, :, c]
        return remote(at, at, send.at[F_C + e], recv.at[F_C + e], sibling)

    def out_core_here(e):
        at = fin.at[(y + 4 - e) % 4, :, 1 - c]
        return remote(at, at, send.at[F_C + e], recv.at[F_C + e], sibling)

    for d in range(1, 8):
        out_z(d).start()
    for e in range(1, 4):
        out_y(e, 0).start()
    dmd = -sc * gap / spread
    dmd_out[:32] = dmd[:, :64]
    dmd_out[32:] = dmd[:, 64:]
    row = lax.broadcasted_iota(jnp.int32, (128, 128), 0)
    col = lax.broadcasted_iota(jnp.int32, (128, 128), 1)
    same_index = jnp.where(row == col, 1.0, 0.0).astype(BF16)

    def turn(e):
        out_core_here(e).wait_recv()
        at_row = (y + 4 - e) % 4
        turned = dot_nt(same_index, fin[at_row].reshape(1280, 128))
        cols = pl.ds(pl.multiple_of(at_row * 1280, 128), 1280)
        turned = turned.astype(BF16)
        in_out[:, cols] = turned[:64]
        out_out[:, cols] = turned[64:]

    for d in ORDER[1:]:
        out_z_here(d).wait_recv()
        for e in range(1, 4):
            out_y(e, d).start()
    out_core(0).start()
    for e in (1, 3, 2):
        for d in range(8):
            out_y_here(e, d).wait_recv()
        out_core(e).start()
        turn({1: 0, 3: 1, 2: 3}[e])
    turn(2)

    for k in range(4):
        @pl.when(jnp.logical_not(target_g_self(k)))
        def _():
            first(k).wait_send()
    for k in range(8):
        @pl.when(jnp.logical_not(target_b_self(k)))
        def _():
            part_copy(k).wait_send()
    for q in range(4):
        weight_copy(q).wait_send()
        weight_forward(q).wait_send()
    for side in range(2):
        for part in range(3):
            key_copy(side, part).wait_send()
    out_copy.wait_send()
    for d in range(1, 8):
        second(d).wait_send()
        along_z(eb, E_Z, d).wait_send()
        vel_copy(d).wait_send()
        along_z(lb, L_Z, d).wait_send()
        piece_copy(d).wait_send()
        out_z(d).wait_send()
    for e in range(1, 4):
        early_y(e).wait_send()
        for d in range(8):
            late_y(e, d).wait_send()
            out_y(e, d).wait_send()
    for e in range(4):
        out_core(e).wait_send()


def window(latent, noise, gen_step, critic_step, gen_in, gen_out_t, embed, out, weight):
    smem = pl.BlockSpec(memory_space=pltpu.SMEM)
    return pl.pallas_call(
        window_kernel,
        out_shape=(
            jax.ShapeDtypeStruct((64, 64), F32),
            jax.ShapeDtypeStruct((64, D), BF16),
            jax.ShapeDtypeStruct((64, D), BF16),
        ),
        in_specs=vmem(2) + [smem, smem] + vmem(4) + [pl.BlockSpec(memory_space=pl.ANY)],
        out_specs=tuple(vmem(3)),
        scratch_shapes=[
            pltpu.VMEM((64, D), F32),
            pltpu.VMEM((32, 128), BF16),
            pltpu.VMEM((8, 4, 32, 128), BF16),
            pltpu.VMEM((4, CHUNK, 3 * HD), BF16),
            pltpu.VMEM((ROWS, 3 * HD), F32),
            pltpu.VMEM((ROWS, 128), F32),
            pltpu.VMEM((ROWS, 2 * HD), BF16),
            pltpu.VMEM((2 * ROWS, 2 * HD), BF16),
            pltpu.VMEM((2 * ROWS, 2 * HD), BF16),
            pltpu.VMEM((2 * HD, 128), BF16),
            pltpu.VMEM((2, 64, 128), BF16),
            pltpu.VMEM((8, 128, 128), BF16),
            pltpu.VMEM((4, 8, 32, 128), BF16),
            pltpu.VMEM((4, 8, 32, 128), BF16),
            pltpu.VMEM((7, 128, 128), BF16),
            pltpu.VMEM((4, 32, 128), F32),
            pltpu.VMEM((8, 32, 128), F32),
            pltpu.VMEM((160, 1024), F32),
            pltpu.VMEM((160, 1024), F32),
            pltpu.VMEM((160, 1024), BF16),
            pltpu.VMEM((2, 88, 128), F32),
            pltpu.VMEM((8, 88, 128), F32),
            pltpu.VMEM((4, 8, 2, 80, 128), BF16),
            pltpu.VMEM((32, 64), F32),
            pltpu.VMEM((160, 128), BF16),
            pltpu.VMEM((160, 128), BF16),
            pltpu.SemaphoreType.DMA((N_SEM,)),
            pltpu.SemaphoreType.DMA((N_SEM,)),
            pltpu.SemaphoreType.DMA((1,)),
        ],
        compiler_params=pltpu.CompilerParams(
            collective_id=0, has_side_effects=True, vmem_limit_bytes=56 << 20
        ),
    )(latent, noise, gen_step, critic_step, gen_in, gen_out_t, embed, out, weight)


def per_device(
    gen_input, noise, gen_step, critic_step, gen_in, gen_out, critic_embed, critic_qkv, critic_out
):
    weight = critic_qkv.reshape(2, CHUNK, 3 * HD)
    dmd, grad_in, grad_out = window(
        gen_input[0], noise[0], gen_step, critic_step, gen_in, gen_out.T, critic_embed[0],
        critic_out[0, 0], weight,
    )
    return (dmd[None], grad_in.astype(F32), grad_out.astype(F32).T)


def solution(mesh):
    return jax.shard_map(
        per_device,
        mesh=mesh,
        in_specs=(
            P("dp", "seq", None),
            P("dp", "seq", None),
            P("dp"),
            P("dp"),
            P(),
            P(),
            P("grp", None, None),
            P("grp", "seq", None, None),
            P("grp", "seq", None, None),
        ),
        out_specs=(P("dp", "seq", None), P(), P()),
        check_vma=False,
    )
```

```python
import jax
import jax.numpy as jnp
from jax import lax
from jax.experimental import pallas as pl
from jax.experimental.pallas import tpu as pltpu
from jax.sharding import PartitionSpec as P

F32 = jnp.float32
BF16 = jnp.bfloat16
NT = 1000
D = 5120
HALF = 2560
LAT = 64
HD = 128
ROWS = 2048
TILE = 256
PART = 320
CHUNK = 1280
SHIFT_VALUE = 5.0
EPS_NORM = 1e-06
EPS_SPREAD = 1e-06
COUNT = 4096 * 64
GA = 0.7978845608028654
GB = GA * 0.044715
SCORE_SCALE = 1.4426950408889634 * HD**-0.5
MESH = pl.DeviceIdType.MESH
CONTRACT_LAST = (((1,), (1,)), ((), ()))


def dot(a, b):
    return jnp.dot(a, b, preferred_element_type=F32)


def dot_nt(a, b):
    return lax.dot_general(a, b, CONTRACT_LAST, preferred_element_type=F32)


def place():
    b = lax.axis_index("grp")
    s = lax.axis_index("seq")
    c = lax.axis_index("dp")
    return b, s // 32, (s // 4) % 8, s % 4, c


def seq_of(xh, z, y):
    return xh * 32 + z * 4 + y


def remote(src, dst, send, recv, device):
    return pltpu.make_async_remote_copy(
        src_ref=src, dst_ref=dst, send_sem=send, recv_sem=recv, device_id=device, device_id_type=MESH
    )


def greet(barrier, device):
    pl.semaphore_signal(barrier, inc=1, device_id=device, device_id_type=MESH)


def sigma_rows(step_ref):
    step = jnp.full((8, 128), step_ref[0], jnp.int32).astype(F32)
    frac = (step + 1.0) / NT
    return (SHIFT_VALUE * frac / (1.0 + (SHIFT_VALUE - 1.0) * frac))[0:1, :]


def split2(value):
    high = value.astype(BF16)
    low = (value - high.astype(F32)).astype(BF16)
    return high, low


def pack(value):
    return jnp.concatenate([value[:32], value[32:]], axis=1)


def vmem(n):
    return [pl.BlockSpec(memory_space=pltpu.VMEM)] * n


def features(x):
    return x + x * jnp.tanh(x * (GA + GB * (x * x)))


ORDER = (0, 1, 7, 2, 6, 3, 5, 4)
STEPS = ((0, 0, 1280), (1, 0, 1280), (2, 0, 640), (3, 0, 640), (2, 640, 640), (3, 640, 640))
W_Y, W_C, U_Y, G_X, G_Z, E_Z, E_Y, K_C = 0, 126, 4, 5, 9, 16, 24, 28
A_Z, B_X, L_Z, L_Y, X_X, F_Z, F_Y, F_C, N_SEM = 34, 42, 50, 58, 82, 90, 98, 122, 130


def window_kernel(
    lat_ref, noise_ref, gs_ref, cs_ref, gin_ref, gout_ref, embed_ref, out_ref, weight_ref,
    dmd_out, in_out, out_out,
    pre_s, mine_s, rows_s, w_s, acc, ssq, qq, kk, vv, uu, um, vel_s,
    eb, lb, arrive_a, part_b, arrive_b, n_s, slope_s, hid_s, piece_s, arrive_x, fin,
    q_s, gi_s, go_s, send, recv, local,
):
    b, xh, z, y, c = place()
    j = y % 2
    y_high = y // 2
    is_self = jnp.logical_and(j == c, y_high == c)
    barrier = pltpu.get_barrier_semaphore()
    me = (b, seq_of(xh, z, y), c)
    sibling = (b, seq_of(xh, z, y), 1 - c)
    partner = (b, seq_of(xh, z, y + 1 - 2 * j), c)

    def at_z(d):
        return (b, seq_of(xh, (z + d) % 8, y), c)

    def at_y(d):
        return (b, seq_of(xh, z, (y + d) % 4), c)

    def at_x(k):
        return ((b + k // 4) % 2, seq_of((xh + k // 2 % 2) % 2, z, y), (c + k % 2) % 2)

    def source_g_self(k):
        return jnp.logical_and(is_self, jnp.logical_and(xh == k // 2, j == k % 2))

    def target_g_self(k):
        return jnp.logical_and(is_self, jnp.logical_and(xh == k // 2, y_high == k % 2))

    def source_b_self(k):
        return jnp.logical_and(target_g_self(k % 4), b == k // 4)

    def target_b_self(k):
        return jnp.logical_and(source_g_self(k % 4), b == k // 4)

    for k in range(4):
        @pl.when(jnp.logical_not(source_g_self(k)))
        def _():
            greet(barrier, (b, seq_of(k // 2, z, 2 * c + k % 2), j))

    for k in range(8):
        @pl.when(jnp.logical_not(source_b_self(k)))
        def _():
            greet(barrier, (k // 4, seq_of(k // 2 % 2, z, c + 2 * (k % 2)), y_high))

    for d in range(1, 8):
        greet(barrier, at_z(d))
        greet(barrier, at_x(d))
    for d in range(1, 4):
        greet(barrier, at_y(d))
    own_weight = pltpu.make_async_copy(weight_ref, w_s.at[pl.ds(0, 2)], local.at[0])
    own_weight.start()

    sg = sigma_rows(gs_ref)
    sc = sigma_rows(cs_ref)
    lat = lat_ref[...]
    um[0] = jnp.concatenate([out_ref[...], jnp.zeros((64, 64), BF16)], axis=1)
    squares = jnp.zeros((64, 128), F32)
    width = 512
    for t in range(D // width):
        cols = slice(t * width, (t + 1) * width)
        pre = dot(lat, gin_ref[:, cols])
        pre_s[:, cols] = pre
        sq = pre * pre
        for u in range(width // 128):
            squares = squares + sq[:, u * 128 : (u + 1) * 128]
    scale = lax.rsqrt(jnp.sum(squares, axis=-1, keepdims=True) / D + EPS_NORM)

    def weight_copy(q):
        rows = pl.ds(q * PART, PART)
        return remote(
            weight_ref.at[c, rows], w_s.at[2, rows], send.at[W_Y + q], recv.at[W_Y + q], partner
        )

    def weight_forward(q):
        rows = pl.ds(q * PART, PART)
        return remote(w_s.at[2, rows], w_s.at[3, rows], send.at[W_C + q], recv.at[W_C + q], sibling)

    out_copy = remote(um.at[0], um.at[1], send.at[U_Y], recv.at[U_Y], partner)

    out = jnp.zeros((64, LAT), F32)
    for t in range(D // width):
        cols = slice(t * width, (t + 1) * width)
        n = pre_s[:, cols] * scale
        th = jnp.tanh(n * (GA + GB * (n * n)))
        out = out + dot_nt((0.5 * n * (1.0 + th)).astype(BF16), gout_ref[:, cols])
    lat_f = lat.astype(F32)
    clean = lat_f - sg[:, :64] * out
    noisy = ((1.0 - sc[:, :64]) * clean + sc[:, :64] * noise_ref[...].astype(F32)).astype(BF16)
    mine = pack(noisy)
    mine_s[...] = mine
    slot = xh * 2 + j

    @pl.when(is_self)
    def _():
        rows_s[0, slot] = mine

    pl.semaphore_wait(barrier, 29 - 2 * is_self.astype(jnp.int32))

    def first(k):
        device = (b, seq_of(k // 2, z, c + 2 * (k % 2)), y_high)
        return remote(mine_s, rows_s.at[0, slot], send.at[G_X + k], recv.at[G_X + slot], device)

    for k in range(4):
        @pl.when(jnp.logical_not(target_g_self(k)))
        def _():
            first(k).start()
    weight_copy(0).start()
    weight_copy(1).start()

    clean = pack(clean)
    high, low = split2(lat_f * scale)
    early = jnp.concatenate([high, low], axis=1)
    eb[0, 0] = jnp.where(b == 0, early[:32], early[32:])

    for k in range(4):
        @pl.when(jnp.logical_not(source_g_self(k)))
        def _():
            remote(mine_s, rows_s.at[0, k], send.at[G_X + k], recv.at[G_X + k], me).wait_recv()

    def second(p):
        d = ORDER[p]
        return remote(
            rows_s.at[0], rows_s.at[p], send.at[G_Z + p - 1], recv.at[G_Z + p - 1], at_z(d)
        )

    for p in range(1, 8):
        second(p).start()

    def along_z(buf, base, d):
        return remote(buf.at[0, 0], buf.at[0, d], send.at[base + d], recv.at[base + d], at_z(d))

    def early_y(d):
        return remote(eb.at[0], eb.at[d], send.at[E_Y + d], recv.at[E_Y + d], at_y(d))

    def late_y(e, d):
        n = L_Y + (e - 1) * 8 + d
        return remote(lb.at[0, d], lb.at[e, d], send.at[n], recv.at[n], at_y(e))

    out_copy.start()
    for d in range(1, 8):
        along_z(eb, E_Z, d).start()
    for q in range(2, 4):
        weight_copy(q).start()

    vv[:, HD:] = jnp.ones((2 * ROWS, HD), BF16)
    own_weight.wait()

    def key_copy(side, part):
        rows = pl.ds(side * 1024, 1024)
        there = pl.ds(ROWS + side * 1024, 1024)
        n = K_C + side * 3 + part
        if part == 2:
            return remote(vv.at[rows, pl.ds(0, HD)], vv.at[there, pl.ds(0, HD)], send.at[n], recv.at[n], sibling)
        return remote(
            kk.at[rows, pl.ds(0, HD)], kk.at[there, pl.ds(part * HD, HD)], send.at[n], recv.at[n], sibling
        )

    starts = (j * HALF, j * HALF + CHUNK, (1 - j) * HALF + c * CHUNK, (1 - j) * HALF + (1 - c) * CHUNK)
    last = len(STEPS) - 1
    for f, (block, low_row, size) in enumerate(STEPS):
        embed = embed_ref[:, pl.ds(pl.multiple_of(starts[block] + low_row, 128), size)]
        if f == 1:
            weight_copy(0).wait_recv()
            weight_forward(0).start()
            for d in range(1, 8):
                along_z(eb, E_Z, d).wait_recv()
            for d in range(1, 4):
                early_y(d).start()
        if f == 2:
            qv = jnp.zeros((64, LAT), F32)
            for t in range(D // width):
                cols = slice(t * width, (t + 1) * width)
                n = pre_s[:, cols] * scale
                n2 = n * n
                th = jnp.tanh(n * (GA + GB * n2))
                slope = 0.5 * (1.0 + th) + 0.5 * n * (1.0 - th * th) * (GA + 3.0 * GB * n2)
                qv = qv + dot_nt((slope * n).astype(BF16), gout_ref[:, cols])
            q_s[...] = jnp.where(b == 0, qv[:32], qv[32:])

            start = (y * 8 + z) * 160
            window = pl.ds(pl.multiple_of(start // 128 * 128, 128), 256)
            row = lax.broadcasted_iota(jnp.int32, (160, 256), 0)
            col = lax.broadcasted_iota(jnp.int32, (160, 256), 1)
            choose = jnp.where(col == row + start % 128, 1.0, 0.0).astype(BF16)
            cut = gin_ref[:, window]
            gi_s[...] = dot_nt(choose, jnp.concatenate([cut, cut], axis=0)).astype(BF16)
            cut = gout_ref[:, window]
            go_s[...] = dot_nt(choose, jnp.concatenate([cut, jnp.zeros_like(cut)], axis=0)).astype(BF16)

            weight_copy(1).wait_recv()
            weight_forward(1).start()
        if f == 3:
            weight_copy(2).wait_recv()
            weight_forward(2).start()
            weight_forward(0).wait_recv()
            weight_forward(1).wait_recv()
        if f == 4:
            weight_copy(3).wait_recv()
            weight_forward(3).start()
        if f == 5:
            weight_forward(2).wait_recv()
            weight_forward(3).wait_recv()

        def activate(t):
            side, part = t // 4, t % 4
            if f == 0 and side == 0:
                for p in (2 * part, 2 * part + 1):
                    if p > 0:
                        second(p).wait_recv()
            tile = rows_s[2 * part : 2 * part + 2].reshape(TILE, 128)
            x = dot(tile[:, side * 64 : (side + 1) * 64], embed)
            e = features(x)
            squares = e * e
            total = squares[:, :128]
            for u in range(1, size // 128):
                total = total + squares[:, u * 128 : (u + 1) * 128]
            rows = slice(t * TILE, (t + 1) * TILE)
            ssq[rows, :] = total if f == 0 else ssq[rows, :] + total
            return e.astype(BF16)

        def accumulate(t, e):
            rows = slice(t * TILE, (t + 1) * TILE)
            got = dot(e, w_s[block, low_row : low_row + size])
            if f > 0:
                got = got + acc[rows, :]
            if f < last:
                acc[rows, :] = got
                return
            mean = jnp.sum(ssq[rows, :], axis=-1, keepdims=True) / D
            got = (got * lax.rsqrt(mean + 4.0 * EPS_NORM)).astype(BF16)
            qq[rows, :] = jnp.concatenate(split2(got[:, :HD].astype(F32) * SCORE_SCALE), axis=1)
            kk[rows, :] = jnp.concatenate([got[:, HD : 2 * HD]] * 2, axis=1)
            vv[rows, :HD] = got[:, 2 * HD :]
            if t % 4 == 3:
                for part in range(3):
                    key_copy(t // 4, part).start()

        before = activate(0)
        for t in range(1, 8):
            now = activate(t)
            accumulate(t - 1, before)
            before = now
        accumulate(7, before)

    out_copy.wait_recv()
    own = um[0][:, :64]
    other = um[1][:, :64]
    full = jnp.concatenate([jnp.where(j == 0, own, other), jnp.where(j == 0, other, own)], axis=0)
    none = jnp.zeros((HD, LAT), BF16)
    uu[:HD, :] = jnp.concatenate([full, none], axis=1)
    uu[HD:, :] = jnp.concatenate([none, full], axis=1)
    for side in range(2):
        for part in range(3):
            key_copy(side, part).wait_recv()

    def vel_copy(p):
        e = (8 - ORDER[p]) % 8
        return remote(vel_s.at[p], arrive_a.at[e - 1], send.at[A_Z + e], recv.at[A_Z + e], at_z(e))

    def scores(p):
        query = jnp.concatenate(
            [qq[p * 128 : (p + 1) * 128, :], qq[1024 + p * 128 : 1024 + (p + 1) * 128, :]], axis=0
        )
        return dot_nt(query, kk[...])

    def mix(s):
        top = jnp.max(s, axis=-1, keepdims=True)
        got = dot(jnp.exp2(s - top).astype(BF16), vv[...])
        attended = (got[:, :HD] / got[:, HD:]).astype(BF16)
        return jnp.concatenate([attended[:128], attended[128:]], axis=1)

    def velocity(p, both):
        vel_s[p] = dot(both, uu[...]).astype(BF16)
        if p > 0:
            vel_copy(p).start()

    s_next = scores(7)
    both = None
    for p in range(7, -1, -1):
        s_now = s_next
        if p > 0:
            s_next = scores(p - 1)
        if both is not None:
            velocity(p + 1, both)
        both = mix(s_now)
    velocity(0, both)

    total = vel_s[0].astype(F32)
    for p in range(7, 0, -1):
        vel_copy(p).wait_recv()
        total = total + arrive_a[(8 - ORDER[p]) % 8 - 1].astype(F32)
    for k in range(4):
        part_b[k] = total[k * 32 : (k + 1) * 32]
    slot_b = b * 4 + xh * 2 + y_high

    def part_copy(k):
        device = (k // 4, seq_of(k // 2 % 2, z, 2 * c + k % 2), j)
        return remote(part_b.at[k % 4], arrive_b.at[slot_b], send.at[B_X + k], recv.at[B_X + slot_b], device)

    for k in range(8):
        @pl.when(jnp.logical_not(target_b_self(k)))
        def _():
            part_copy(k).start()

        @pl.when(target_b_self(k))
        def _():
            arrive_b[slot_b] = part_b[k % 4]

    for d in range(1, 4):
        early_y(d).wait_recv()
    early = eb[...].reshape(1024, 128)
    n = dot_nt(gi_s[...], early)
    n2 = n * n
    th = jnp.tanh(n * (GA + GB * n2))
    n_s[...] = n
    hid_s[...] = (0.5 * n * (1.0 + th)).astype(BF16)
    slope_s[...] = 0.5 * (1.0 + th) + 0.5 * n * (1.0 - th * th) * (GA + 3.0 * GB * n2)

    for k in range(8):
        @pl.when(jnp.logical_not(source_b_self(k)))
        def _():
            remote(
                part_b.at[k % 4], arrive_b.at[k], send.at[B_X + k], recv.at[B_X + k], me
            ).wait_recv()

    teacher = arrive_b[0] + arrive_b[1] + arrive_b[2] + arrive_b[3]
    fake = arrive_b[4] + arrive_b[5] + arrive_b[6] + arrive_b[7]
    gap = fake - teacher
    away = jnp.abs(clean - (mine_s[...].astype(F32) - sc * teacher))
    my_gap = jnp.where(b == 0, gap[:, :64], gap[:, 64:])
    my_away = jnp.where(b == 0, away[:, :64], away[:, 64:])
    away_row = jnp.sum(my_away, axis=-1, keepdims=True)
    rbar = jnp.sum(my_gap * q_s[...], axis=-1, keepdims=True) / D
    r_high, r_low = split2(rbar)
    a_high, a_low = split2(away_row)
    a_rest = (away_row - a_high.astype(F32) - a_low.astype(F32)).astype(BF16)
    lane = lax.broadcasted_iota(jnp.int32, (32, 64), 1)
    extra = jnp.zeros((32, 64), F32)
    for at, value in enumerate((r_high, r_low, a_high, a_low, a_rest)):
        extra = jnp.where(lane == at, value.astype(F32), extra)
    lb[0, 0] = jnp.concatenate([my_gap, extra], axis=1).astype(BF16)

    for d in range(1, 8):
        along_z(lb, L_Z, d).start()
    for e in range(1, 4):
        late_y(e, 0).start()
    for d in ORDER[1:]:
        along_z(lb, L_Z, d).wait_recv()
        for e in range(1, 4):
            late_y(e, d).start()
    for d in range(8):
        for e in range(1, 4):
            late_y(e, d).wait_recv()
    late = lb[...].reshape(1024, 128)
    lane = lax.broadcasted_iota(jnp.int32, (16, 128), 1)
    pick = jnp.where(jnp.logical_or(lane == 64, lane == 65), 1.0, 0.0).astype(BF16)
    rbar_all = dot_nt(pick, late)[0:1, :]
    away_all = dot(jnp.ones((16, 1024), BF16), late)[0:1, :]
    lane1 = lax.broadcasted_iota(jnp.int32, (1, 128), 1)
    away_sum = jnp.sum(
        jnp.where(jnp.logical_and(lane1 >= 66, lane1 <= 68), away_all, 0.0), axis=-1, keepdims=True
    )
    dpre = (slope_s[...] * dot_nt(go_s[...], late) - n_s[...] * rbar_all).astype(BF16)
    grad_in = dot(dpre, early)
    grad_out = dot(hid_s[...], late)
    piece = jnp.concatenate([grad_in[:, :64] + grad_in[:, 64:], grad_out[:, :64]], axis=1)
    row8 = lax.broadcasted_iota(jnp.int32, (8, 128), 0)
    extra8 = jnp.where(row8 == 0, away_sum, sg * sc)
    for p in range(2):
        piece_s[p, :80] = piece[p * 80 : (p + 1) * 80]
        piece_s[p, 80:] = extra8

    def piece_copy(k):
        return remote(
            piece_s.at[(c + k % 2) % 2], arrive_x.at[k], send.at[X_X + k], recv.at[X_X + k], at_x(k)
        )

    for k in range(1, 8):
        piece_copy(k).start()
    arrive_x[0] = piece_s[c]
    for k in range(1, 8):
        piece_copy(k).wait_recv()
    same = arrive_x[0] + arrive_x[2] + arrive_x[4] + arrive_x[6]
    cross = arrive_x[1] + arrive_x[3] + arrive_x[5] + arrive_x[7]
    spread = same[80:81] / COUNT + EPS_SPREAD
    spread_cross = cross[80:81] / COUNT + EPS_SPREAD
    result = (0.25 * same[81:82] / spread) * same[:80] + (0.25 * cross[81:82] / spread_cross) * cross[:80]
    fin[y, z, c] = result.astype(BF16)

    def out_z(d):
        at = fin.at[y, z, c]
        return remote(at, at, send.at[F_Z + d], recv.at[F_Z + d], at_z(d))

    def out_z_here(d):
        at = fin.at[y, (z + 8 - d) % 8, c]
        return remote(at, at, send.at[F_Z + d], recv.at[F_Z + d], at_z(d))

    def out_y(e, d):
        n = F_Y + (e - 1) * 8 + d
        at = fin.at[y, (z + 8 - d) % 8, c]
        return remote(at, at, send.at[n], recv.at[n], at_y(e))

    def out_y_here(e, d):
        n = F_Y + (e - 1) * 8 + d
        at = fin.at[(y + 4 - e) % 4, (z + 8 - d) % 8, c]
        return remote(at, at, send.at[n], recv.at[n], at_y(e))

    def out_core(e):
        at = fin.at[(y + 4 - e) % 4, :, c]
        return remote(at, at, send.at[F_C + e], recv.at[F_C + e], sibling)

    def out_core_here(e):
        at = fin.at[(y + 4 - e) % 4, :, 1 - c]
        return remote(at, at, send.at[F_C + e], recv.at[F_C + e], sibling)

    for d in range(1, 8):
        out_z(d).start()
    for e in range(1, 4):
        out_y(e, 0).start()
    dmd = -sc * gap / spread
    dmd_out[:32] = dmd[:, :64]
    dmd_out[32:] = dmd[:, 64:]
    row = lax.broadcasted_iota(jnp.int32, (128, 128), 0)
    col = lax.broadcasted_iota(jnp.int32, (128, 128), 1)
    same_index = jnp.where(row == col, 1.0, 0.0).astype(BF16)

    def turn(e):
        out_core_here(e).wait_recv()
        at_row = (y + 4 - e) % 4
        turned = dot_nt(same_index, fin[at_row].reshape(1280, 128))
        cols = pl.ds(pl.multiple_of(at_row * 1280, 128), 1280)
        turned = turned.astype(BF16)
        in_out[:, cols] = turned[:64]
        out_out[:, cols] = turned[64:]

    for d in ORDER[1:]:
        out_z_here(d).wait_recv()
        for e in range(1, 4):
            out_y(e, d).start()
    out_core(0).start()
    for e in (1, 3, 2):
        for d in range(8):
            out_y_here(e, d).wait_recv()
        out_core(e).start()
        turn({1: 0, 3: 1, 2: 3}[e])
    turn(2)

    for k in range(4):
        @pl.when(jnp.logical_not(target_g_self(k)))
        def _():
            first(k).wait_send()
    for k in range(8):
        @pl.when(jnp.logical_not(target_b_self(k)))
        def _():
            part_copy(k).wait_send()
    for q in range(4):
        weight_copy(q).wait_send()
        weight_forward(q).wait_send()
    for side in range(2):
        for part in range(3):
            key_copy(side, part).wait_send()
    out_copy.wait_send()
    for d in range(1, 8):
        second(d).wait_send()
        along_z(eb, E_Z, d).wait_send()
        vel_copy(d).wait_send()
        along_z(lb, L_Z, d).wait_send()
        piece_copy(d).wait_send()
        out_z(d).wait_send()
    for e in range(1, 4):
        early_y(e).wait_send()
        for d in range(8):
            late_y(e, d).wait_send()
            out_y(e, d).wait_send()
    for e in range(4):
        out_core(e).wait_send()


def window(latent, noise, gen_step, critic_step, gen_in, gen_out_t, embed, out, weight):
    smem = pl.BlockSpec(memory_space=pltpu.SMEM)
    return pl.pallas_call(
        window_kernel,
        out_shape=(
            jax.ShapeDtypeStruct((64, 64), F32),
            jax.ShapeDtypeStruct((64, D), BF16),
            jax.ShapeDtypeStruct((64, D), BF16),
        ),
        in_specs=vmem(2) + [smem, smem] + vmem(4) + [pl.BlockSpec(memory_space=pl.ANY)],
        out_specs=tuple(vmem(3)),
        scratch_shapes=[
            pltpu.VMEM((64, D), F32),
            pltpu.VMEM((32, 128), BF16),
            pltpu.VMEM((8, 4, 32, 128), BF16),
            pltpu.VMEM((4, CHUNK, 3 * HD), BF16),
            pltpu.VMEM((ROWS, 3 * HD), F32),
            pltpu.VMEM((ROWS, 128), F32),
            pltpu.VMEM((ROWS, 2 * HD), BF16),
            pltpu.VMEM((2 * ROWS, 2 * HD), BF16),
            pltpu.VMEM((2 * ROWS, 2 * HD), BF16),
            pltpu.VMEM((2 * HD, 128), BF16),
            pltpu.VMEM((2, 64, 128), BF16),
            pltpu.VMEM((8, 128, 128), BF16),
            pltpu.VMEM((4, 8, 32, 128), BF16),
            pltpu.VMEM((4, 8, 32, 128), BF16),
            pltpu.VMEM((7, 128, 128), BF16),
            pltpu.VMEM((4, 32, 128), F32),
            pltpu.VMEM((8, 32, 128), F32),
            pltpu.VMEM((160, 1024), F32),
            pltpu.VMEM((160, 1024), F32),
            pltpu.VMEM((160, 1024), BF16),
            pltpu.VMEM((2, 88, 128), F32),
            pltpu.VMEM((8, 88, 128), F32),
            pltpu.VMEM((4, 8, 2, 80, 128), BF16),
            pltpu.VMEM((32, 64), F32),
            pltpu.VMEM((160, 128), BF16),
            pltpu.VMEM((160, 128), BF16),
            pltpu.SemaphoreType.DMA((N_SEM,)),
            pltpu.SemaphoreType.DMA((N_SEM,)),
            pltpu.SemaphoreType.DMA((1,)),
        ],
        compiler_params=pltpu.CompilerParams(
            collective_id=0, has_side_effects=True, vmem_limit_bytes=56 << 20
        ),
    )(latent, noise, gen_step, critic_step, gen_in, gen_out_t, embed, out, weight)


def per_device(
    gen_input, noise, gen_step, critic_step, gen_in, gen_out, critic_embed, critic_qkv, critic_out
):
    weight = critic_qkv.reshape(2, CHUNK, 3 * HD)
    dmd, grad_in, grad_out = window(
        gen_input[0], noise[0], gen_step, critic_step, gen_in, gen_out.T, critic_embed[0],
        critic_out[0, 0], weight,
    )
    return (dmd[None], grad_in.astype(F32), grad_out.astype(F32).T)


def solution(mesh):
    return jax.shard_map(
        per_device,
        mesh=mesh,
        in_specs=(
            P("dp", "seq", None),
            P("dp", "seq", None),
            P("dp"),
            P("dp"),
            P(),
            P(),
            P("grp", None, None),
            P("grp", "seq", None, None),
            P("grp", "seq", None, None),
        ),
        out_specs=(P("dp", "seq", None), P(), P()),
        check_vma=False,
    )
```
